32 devices in a mesh: rep: 4 (over z), pipe: 4 (over y, x), tp: 2 (over core).
Axes of the slice: x: 2, y: 2, z: 4, core: 2. Of those that a mesh axis runs over, the one named last changes fastest.
Arguments:
- fwd_in: bfloat16 [4, 4, 256, 3072], P('rep', 'pipe', None, 'tp'), may hold values from -6 to 6
- bwd_in: bfloat16 [4, 4, 256, 3072], P('rep', 'pipe', None, 'tp'), may hold values from -6 to 6
- bwd_grad: bfloat16 [4, 4, 256, 3072], P('rep', 'pipe', None, 'tp'), may hold values from -18 to 18
- seg_fwd: int32 [4, 4, 256], P('rep', 'pipe'), may hold values from 0 to 3, never falling along the last dimension, each value on 1 to 128 neighbouring positions
- seg_bwd: int32 [4, 4, 256], P('rep', 'pipe'), may hold values from 0 to 3, never falling along the last dimension, each value on 1 to 128 neighbouring positions
- w_query: bfloat16 [4, 4, 3072, 3072], P('rep', 'pipe', None, 'tp'), may hold values from -6 to 6
- w_key: bfloat16 [4, 4, 3072, 128], P('rep', 'pipe'), may hold values from -60 to 60
- gain: bfloat16 [4, 4, 3072], P('rep', 'pipe', 'tp'), may hold values from 0.5 to 1.5
- gossip_exp: int32 [4], P('pipe'), may hold values from 0 to 1
Outputs:
- next_input: bfloat16 [4, 4, 256, 3072], P('rep', 'pipe', None, 'tp')
- prev_grad: bfloat16 [4, 4, 256, 3072], P('rep', 'pipe', None, 'tp')
- w_query_out: bfloat16 [4, 4, 3072, 3072], P('rep', 'pipe', None, 'tp')
- w_key_out: bfloat16 [4, 4, 3072, 128], P('rep', 'pipe')
- gain_out: bfloat16 [4, 4, 3072], P('rep', 'pipe', 'tp')
The draws below stay inside these ranges and needn't reach their ends.
Inputs may be any that keep to these rules, and one draw needn't show every extreme that they name: The partner of replica r at section p is r XOR 2^k with k = gossip_exp[p]. `seg_fwd`: along each section's rows the caption ids never fall; each caption has 1 to 128 tokens. `seg_bwd`: along each section's rows the caption ids never fall; each caption has 1 to 128 tokens.
All inputs are finite; a program needn't handle non-finite values.
Results may differ from the reference program's by a relative error of at most 0.015.
The reference program's roundings to bfloat16 on the way count: a program that leaves them out, or rounds other values in their place, can miss the bound.
Values may be sent and summed in bfloat16 or wider, within the bound.
No kernel may reach another device: no remote copies, remote signals or barrier semaphores. Data moves between devices by JAX's collectives and lax.ppermute only.
A program may use at most 192 MiB of HBM per device.

```python
import math
import jax
import jax.numpy as jnp
import numpy as np
from jax import lax

HEAD = 128
HEADS = 24
D = 3072
ROWS = 256
CAPTIONS = 4
CAP_MOST = 128
REPLICAS = 4
SECTIONS = 4
N_REP = 4


def draw_w_query(key, part):
    leading = jax.random.normal(jax.random.fold_in(key, 11), (REPLICAS, SECTIONS, D, HEAD), jnp.float32)
    others = jax.random.normal(jax.random.fold_in(key, 12), (REPLICAS, SECTIONS, D, D - HEAD), jnp.float32)
    return jnp.clip(jnp.concatenate([leading, others], axis=3), -6.0, 6.0).astype(jnp.bfloat16)


def draw_w_key(key, part):
    base = jnp.clip(jax.random.normal(jax.random.fold_in(key, 13), (REPLICAS, SECTIONS, D, HEAD), jnp.float32), -6.0, 6.0)
    return base.astype(jnp.bfloat16)


def draw_bwd_grad(key, part):
    shape = (REPLICAS, SECTIONS, ROWS, D)
    ramp = jnp.arange(SECTIONS, dtype=jnp.float32) / max(SECTIONS - 1, 1)
    noise = jnp.clip(jax.random.normal(jax.random.fold_in(key, 22), shape, jnp.float32), -6.0, 6.0)
    factor = 1.0 + 2.0 * ramp
    return (noise * factor[None, :, None, None]).astype(jnp.bfloat16)


def with_ends(array, rng, least, high):
    longest = array.shape.index(max(array.shape))
    spots = []
    for shift in (0, 1):
        where = [jax.random.randint(jax.random.fold_in(rng, axis), (), 0, length) for axis, length in enumerate(array.shape)]
        where[longest] = (where[longest] + shift) % array.shape[longest]
        spots.append(tuple(where))
    return array.at[spots[0]].set(least).at[spots[1]].set(high)


def levels(key, shape, shards, least, top_value):
    loudness = 1.0
    for axis_at, blocks in shards:
        draws = jax.random.uniform(jax.random.fold_in(jax.random.fold_in(key, 6), axis_at), (blocks,), jnp.float32, least / len(shards), top_value / len(shards))
        loudness = loudness * jnp.repeat(jnp.exp(draws), shape[axis_at] // blocks).reshape((-1,) + (1,) * (len(shape) - 1 - axis_at))
    return loudness


def profile(amount, total, limit, lean):
    loads = [(1 << 20) // math.isqrt(grade ** lean) + 1 for grade in range(2, amount + 1)]
    rest, counts = total - limit - (amount - 1), [1] * (amount - 1)
    while rest > 0:
        movable = [i for i in range(amount - 1) if counts[i] < limit]
        pool, budget = sum([loads[i] for i in movable]), rest
        for i in movable:
            addition = min(limit - counts[i], max(1, budget * loads[i] // pool), rest)
            counts[i] = counts[i] + addition
            rest = rest - addition
    return np.array([limit] + counts)


def ragged(stream_key, amount, total, most, skew):
    if amount == 2:
        one = jax.random.randint(stream_key, (), max(1, total - most), min(most, total - 1) + 1)
        return jnp.stack([one, total - one])
    tallies = jnp.asarray(profile(amount, total, most, skew), jnp.int32)
    twos = (amount - 1) // 2
    giver, receiver = tallies[1:1 + 2 * twos:2], tallies[2:2 + 2 * twos:2]
    slack = jnp.minimum(giver - 1, most - receiver)
    moved = jax.random.randint(jax.random.fold_in(stream_key, 1), (twos,), 0, 1 << 20) % (slack + 1)
    tallies = tallies.at[1:1 + 2 * twos:2].set(giver - moved).at[2:2 + 2 * twos:2].set(receiver + moved)
    return tallies[jax.random.permutation(jax.random.fold_in(stream_key, 2), amount)]


def scatter_about(key, shape, width, reach, pieces=(), kind=jnp.bfloat16):
    entries = width * jax.random.normal(key, shape, jnp.float32)
    if pieces:
        entries = entries * levels(key, shape, pieces, -0.22, 0.18)
    return jnp.clip(entries, -reach, reach).astype(kind)


def setup_inputs(seed: int = 0) -> dict:
    seeds = jax.random.split(jax.random.key(seed), 10)
    return {
        "fwd_in": scatter_about(seeds[0], (REPLICAS, SECTIONS, ROWS, D), 1.0, 6.0, ((0, 4), (1, 4), (3, 2))),
        "bwd_in": scatter_about(seeds[1], (REPLICAS, SECTIONS, ROWS, D), 1.0, 6.0, ((0, 4), (1, 4), (3, 2))),
        "bwd_grad": draw_bwd_grad(jax.random.fold_in(seeds[9], 71), 0),
        "seg_fwd": jax.vmap(lambda own: jnp.searchsorted(jnp.cumsum(ragged(own, CAPTIONS, ROWS, CAP_MOST, 1)), jnp.arange(ROWS), side="right"))(jax.random.split(seeds[3], REPLICAS * SECTIONS)).reshape((REPLICAS, SECTIONS, ROWS)).astype(jnp.int32),
        "seg_bwd": jax.vmap(lambda own: jnp.searchsorted(jnp.cumsum(ragged(own, CAPTIONS, ROWS, CAP_MOST, 1)), jnp.arange(ROWS), side="right"))(jax.random.split(seeds[4], REPLICAS * SECTIONS)).reshape((REPLICAS, SECTIONS, ROWS)).astype(jnp.int32),
        "w_query": draw_w_query(jax.random.fold_in(seeds[9], 71), 0),
        "w_key": draw_w_key(jax.random.fold_in(seeds[9], 71), 0),
        "gain": jnp.clip(1.0 + 0.1 * jax.random.normal(seeds[7], (REPLICAS, SECTIONS, D), jnp.float32), 0.5, 1.5).astype(jnp.bfloat16),
        "gossip_exp": with_ends(jax.random.randint(seeds[8], (SECTIONS,), 0, N_REP // 4 + 1), jax.random.fold_in(seeds[8], 1), 0, (N_REP // 4 + 1) - 1).astype(jnp.int32),
    }


LN_EPS = 1e-05
STEP_EPS = 1e-06
LEARN_RATE = 0.2
MASK_FILL = -1e+30

def normalize(rows, gain_row):
    values = rows.astype(jnp.float32)
    centred = values - lax.optimization_barrier(jnp.mean(values, axis=-1, keepdims=True))
    inv_std = lax.rsqrt(lax.optimization_barrier(jnp.mean(centred * centred, axis=-1, keepdims=True)) + LN_EPS)
    scaled = centred * inv_std
    normed = (scaled * gain_row.astype(jnp.float32)).astype(jnp.bfloat16)
    return (values, scaled, inv_std, normed)

def attend(normed, caption, query_weight, key_weight):
    in_scale = D ** (-0.5)
    count = normed.shape[0]
    queries = (jnp.dot(normed, query_weight, preferred_element_type=jnp.float32) * in_scale).astype(jnp.bfloat16)
    keys = (jnp.dot(normed, key_weight, preferred_element_type=jnp.float32) * in_scale).astype(jnp.bfloat16)
    query_heads = queries.reshape(count, HEADS, HEAD).astype(jnp.float32)
    value_heads = normed.reshape(count, HEADS, HEAD).astype(jnp.float32)
    key_rows = keys.astype(jnp.float32)
    scores = jnp.einsum('rhd,sd->hrs', query_heads, key_rows) * HEAD ** (-0.5)
    same = caption[:, None] == caption[None, :]
    scores = jnp.where(same[None], scores, MASK_FILL)
    peak = lax.optimization_barrier(jnp.max(scores, axis=-1, keepdims=True))
    expo = jnp.exp(scores - peak)
    probs = (expo / lax.optimization_barrier(jnp.sum(expo, axis=-1, keepdims=True))).astype(jnp.bfloat16)
    mixed = jnp.einsum('hrs,shd->rhd', probs.astype(jnp.float32), value_heads).reshape(count, D)
    return (query_heads, key_rows, value_heads, probs, mixed)

def section(items):
    fwd_rows, bwd_rows, grad_rows, seg_fwd, seg_bwd, query_weight, key_weight, gain_row = items
    in_scale = D ** (-0.5)
    count = fwd_rows.shape[0]
    values, scaled, inv_std, normed = normalize(fwd_rows, gain_row)
    mixed = attend(normed, seg_fwd, query_weight, key_weight)[4]
    section_out = (values + mixed).astype(jnp.bfloat16)
    values_b, scaled_b, inv_b, normed_b = normalize(bwd_rows, gain_row)
    query_heads, key_rows, value_heads, probs, unused = attend(normed_b, seg_bwd, query_weight, key_weight)
    grad_heads = grad_rows.astype(jnp.float32).reshape(count, HEADS, HEAD)
    prob_f = probs.astype(jnp.float32)
    value_grad = jnp.einsum('hrs,rhd->shd', prob_f, grad_heads).reshape(count, D)
    prob_grad = jnp.einsum('rhd,shd->hrs', grad_heads, value_heads)
    score_grad = (prob_f * (prob_grad - lax.optimization_barrier(jnp.sum(prob_grad * prob_f, axis=-1, keepdims=True))) * HEAD ** (-0.5)).astype(jnp.bfloat16)
    score_f = score_grad.astype(jnp.float32)
    query_grad = jnp.einsum('hrs,sd->rhd', score_f, key_rows).reshape(count, D).astype(jnp.bfloat16)
    key_grad = jnp.einsum('hrs,rhd->sd', score_f, query_heads).astype(jnp.bfloat16)
    normed_grad = (jnp.dot(query_grad, query_weight.T, preferred_element_type=jnp.float32) + jnp.dot(key_grad, key_weight.T, preferred_element_type=jnp.float32)) * in_scale + value_grad
    scaled_grad = normed_grad * gain_row.astype(jnp.float32)
    input_grad = inv_b * (scaled_grad - lax.optimization_barrier(jnp.mean(scaled_grad, axis=-1, keepdims=True)) - scaled_b * lax.optimization_barrier(jnp.mean(scaled_grad * scaled_b, axis=-1, keepdims=True)))
    back_rows = (grad_rows.astype(jnp.float32) + input_grad).astype(jnp.bfloat16)
    grad_query = jnp.dot(normed_b.T, query_grad, preferred_element_type=jnp.float32) * in_scale
    grad_key = jnp.dot(normed_b.T, key_grad, preferred_element_type=jnp.float32) * in_scale
    grad_gain = lax.optimization_barrier(jnp.sum(normed_grad * scaled_b, axis=0))
    squares = jnp.sum(grad_query * grad_query) + jnp.sum(grad_key * grad_key) + jnp.sum(grad_gain * grad_gain)
    return (section_out, back_rows, grad_query, grad_key, grad_gain, squares)

def replica_step(items):
    outs = lax.map(section, items)
    section_out, back_rows, grad_query, grad_key, grad_gain, squares = outs
    total = SECTIONS * (D * D + D * HEAD + D)
    inverse = lax.rsqrt(jnp.sum(squares) / total + STEP_EPS)
    step_query = (LEARN_RATE * grad_query * inverse).astype(jnp.bfloat16)
    step_key = (LEARN_RATE * grad_key * inverse).astype(jnp.bfloat16)
    step_gain = (LEARN_RATE * grad_gain * inverse).astype(jnp.bfloat16)
    return (section_out, back_rows, step_query, step_key, step_gain)

def updated(weight, step):
    return (weight.astype(jnp.float32) - step.astype(jnp.float32)).astype(jnp.bfloat16)

def average(own, partner, own_step, partner_step):
    mine = updated(own, own_step).astype(jnp.float32)
    theirs = updated(partner, partner_step).astype(jnp.float32)
    return ((mine + theirs) * 0.5).astype(jnp.bfloat16)

def reference(fwd_in, bwd_in, bwd_grad, seg_fwd, seg_bwd, w_query, w_key, gain, gossip_exp):
    section_out, back_rows, step_query, step_key, step_gain = lax.map(replica_step, (fwd_in, bwd_in, bwd_grad, seg_fwd, seg_bwd, w_query, w_key, gain))
    next_input = jnp.roll(section_out, 1, axis=1)
    prev_grad = jnp.roll(back_rows, -1, axis=1)
    distance = jnp.left_shift(jnp.int32(1), gossip_exp.astype(jnp.int32))
    section_ids = jnp.arange(SECTIONS, dtype=jnp.int32)

    def combine(index):
        others = jnp.bitwise_xor(index, distance).astype(jnp.int32)
        return (average(w_query[index], w_query[others, section_ids], step_query[index], step_query[others, section_ids]), average(w_key[index], w_key[others, section_ids], step_key[index], step_key[others, section_ids]), average(gain[index], gain[others, section_ids], step_gain[index], step_gain[others, section_ids]))
    w_query_out, w_key_out, gain_out = lax.map(combine, jnp.arange(REPLICAS, dtype=jnp.int32))
    return (next_input, prev_grad, w_query_out, w_key_out, gain_out)
```

```python
import math
from functools import partial

import jax
import jax.numpy as jnp
from jax import lax
from jax.sharding import PartitionSpec as P

HEAD = 128
LN_EPS = 1e-05
STEP_EPS = 1e-06
LEARN_RATE = 0.2
MASK_FILL = -1e30
MOST_BRANCHES = 16
PIECES = 12
F32 = jnp.float32
BF16 = jnp.bfloat16
LAST = (((1,), (1,)), ((), ()))
FIRST = (((0,), (0,)), ((), ()))


def shifted(block, axis, by):
    length = lax.axis_size(axis)
    return lax.ppermute(block, axis, [(i, (i + by) % length) for i in range(length)])


def total_over(value, axis):
    parts = [shifted(value, axis, by) for by in range(1, lax.axis_size(axis))]
    for part in parts:
        value = value + part
    return value


def in_order(mine, other, axis):
    first = lax.axis_index("tp") == 0
    return jnp.where(
        first,
        jnp.concatenate([mine, other], axis=axis),
        jnp.concatenate([other, mine], axis=axis),
    )


def gathered(block, axis):
    return in_order(block, shifted(block, "tp", 1), axis)


def normalize(rows, gain_full):
    values = rows.astype(F32)
    centred = values - jnp.mean(values, axis=-1, keepdims=True)
    inv_std = lax.rsqrt(jnp.mean(centred * centred, axis=-1, keepdims=True) + LN_EPS)
    scaled = centred * inv_std
    normed = (scaled * gain_full.astype(F32)).astype(BF16)
    return scaled, inv_std, normed


def attend(normed, caption, query_weight, key_weight):
    in_scale = normed.shape[1] ** (-0.5)
    count = normed.shape[0]
    heads = query_weight.shape[1] // HEAD
    queries = (jnp.dot(normed, query_weight, preferred_element_type=F32) * in_scale).astype(BF16)
    keys = (jnp.dot(normed, key_weight, preferred_element_type=F32) * in_scale).astype(BF16)
    query_heads = queries.reshape(count, heads, HEAD)
    scores = jnp.einsum("rhd,sd->hrs", query_heads, keys, preferred_element_type=F32) * HEAD ** (-0.5)
    same = caption[:, None] == caption[None, :]
    scores = jnp.where(same[None], scores, MASK_FILL)
    peak = jnp.max(scores, axis=-1, keepdims=True)
    expo = jnp.exp(scores - peak)
    probs = (expo / jnp.sum(expo, axis=-1, keepdims=True)).astype(BF16)
    return query_heads, keys, probs


def updated(weight, grad, inverse):
    step = (LEARN_RATE * grad * inverse).astype(BF16)
    return (weight.astype(F32) - step.astype(F32)).astype(BF16)


def halves(mine, theirs):
    return ((mine.astype(F32) + theirs.astype(F32)) * 0.5).astype(BF16)


def beside(first, second):
    apart = first ^ second
    return apart != 0 and apart & (apart - 1) == 0


def pairings(exponents):
    far = [p for p, k in enumerate(exponents) if k == 1]
    near = [p for p, k in enumerate(exponents) if k == 0]
    best = []

    def search(at, taken, made):
        nonlocal best
        if len(made) > len(best):
            best = list(made)
        if at == len(far):
            return
        search(at + 1, taken, made)
        for other in near:
            if other not in taken and beside(far[at], other):
                search(at + 1, taken | {other}, made + [(far[at], other)])

    search(0, frozenset(), [])
    return best


def routes(exponents, rep_count):
    def at(r, p):
        return r * len(exponents) + p

    trade, send, paired = [], [], set()
    for far, near in pairings(exponents) if rep_count == 4 else []:
        paired |= {far, near}
        for own, other in ((far, near), (near, far)):
            trade += [(at(r, own), at(r, own)) for r in (0, 3)]
            trade += [(at(r, own), at(r, other)) for r in (1, 2)]
        send += [(at(0, far), at(2, far)), (at(3, far), at(1, far))]
        send += [(at(0, near), at(1, near)), (at(3, near), at(2, near))]
        send += [(at(1, far), at(0, near)), (at(2, far), at(3, near))]
        send += [(at(1, near), at(3, far)), (at(2, near), at(0, far))]
    for p, k in enumerate(exponents):
        if p not in paired:
            trade += [(at(r, p), at(r, p)) for r in range(rep_count)]
            send += [(at(r, p), at(r ^ 1 << k, p)) for r in range(rep_count)]
    return (trade if paired else None), send, ("rep", "pipe")


def straight(level, rep_count):
    route = []
    for low in range(rep_count):
        if low ^ 1 << level < rep_count:
            route.append((low, low ^ 1 << level))
    return None, route, "rep"


def exchanged(chains, plan):
    trade, send, axes = plan
    received = []
    for blocks in chains:
        back, moved, landed = [], None, None
        for step in range(len(blocks) + 1):
            going = blocks[step] if step < len(blocks) else None
            held = lax.optimization_barrier([b for b in (going, moved, landed) if b is not None])
            if going is not None:
                going = held.pop(0)
            if moved is not None:
                moved = held.pop(0)
            if landed is not None:
                back.append(held.pop(0))
            landed = None if moved is None else lax.ppermute(moved, axes, send)
            if going is not None:
                going = going if trade is None else lax.ppermute(going, axes, trade)
            moved = going
        back.append(landed)
        received.append(back)
    return received


def finish(values, plan, along):
    (fwd_rows, fwd_other, grad_rows, seg_fwd, query_weight, key_weight, gain_local, gain_full) = values[:8]
    (normed_b, scaled_own, inv_b, query_grad, key_grad, normed_grad, grad_gain, inverse) = values[8:]
    count, local_width = fwd_rows.shape
    width = local_width * lax.axis_size("tp")
    in_scale = width ** (-0.5)
    offset = lax.axis_index("tp") * local_width

    piece = width // PIECES
    sizes = [piece // 2] + [piece] * (PIECES - 1) + [piece // 2]
    spots = [sum(sizes[:i]) for i in range(len(sizes))]

    def stepped(start, size):
        part = lax.slice_in_dim(normed_b, start, start + size, axis=1)
        grad = lax.dot_general(part, query_grad, FIRST, preferred_element_type=F32) * in_scale
        return updated(lax.slice_in_dim(query_weight, start, start + size, axis=0), grad, inverse)

    own = [stepped(start, size) for start, size in zip(spots, sizes)]
    half_normed = lax.dynamic_slice_in_dim(normed_b, offset, local_width, 1)
    grad_key = lax.dot_general(half_normed, key_grad, FIRST, preferred_element_type=F32) * in_scale
    own_key = updated(lax.dynamic_slice_in_dim(key_weight, offset, local_width, 0), grad_key, inverse)
    own_gain = updated(gain_local, grad_gain, inverse).reshape(-1, HEAD)
    rest = jnp.zeros((-own_gain.shape[0] % 16, HEAD), BF16)
    small = jnp.concatenate([own_key, own_gain, rest], axis=0)

    theirs_a, theirs_b = exchanged([own[0::2], own[1::2] + [small]], plan)
    theirs = [None] * len(own)
    theirs[0::2] = theirs_a
    theirs[1::2] = theirs_b[:-1]
    query_out = jnp.concatenate([halves(a, b) for a, b in zip(own, theirs)], axis=0)
    small_out = halves(small, theirs_b[-1])
    key_out = gathered(small_out[:local_width], 0)
    gain_out = small_out[local_width : local_width + own_gain.shape[0]].reshape(-1)

    weighted = normed_grad * gain_local.astype(F32)
    sums = jnp.stack([jnp.sum(weighted, axis=-1), jnp.sum(weighted * scaled_own, axis=-1)])
    sums = total_over(sums, "tp") / width
    input_grad = inv_b * (weighted - sums[0][:, None] - scaled_own * sums[1][:, None])
    back_rows = (grad_rows.astype(F32) + input_grad).astype(BF16)

    normed = normalize(in_order(fwd_rows, fwd_other, 1), gain_full)[2]
    probs = attend(normed, seg_fwd, query_weight, key_weight)[2]
    value_heads = lax.dynamic_slice_in_dim(normed, offset, local_width, 1).reshape(count, -1, HEAD)
    mixed = jnp.einsum("hrs,shd->rhd", probs, value_heads, preferred_element_type=F32)
    section_out = (fwd_rows.astype(F32) + mixed.reshape(count, -1)).astype(BF16)
    if along:
        section_out = shifted(section_out, "pipe", 1)
        back_rows = shifted(back_rows, "pipe", -1)
    return section_out, back_rows, query_out, key_out, gain_out


def shards(fwd_in, bwd_in, bwd_grad, seg_fwd, seg_bwd, w_query, w_key, gain, gossip_exp):
    query_weight = w_query[0, 0]
    key_weight = w_key[0, 0]
    gain_local = gain[0, 0]
    fwd_rows = fwd_in[0, 0]
    grad_rows = bwd_grad[0, 0]
    count, local_width = fwd_rows.shape
    heads = local_width // HEAD
    tp_count = lax.axis_size("tp")
    pipe_count = lax.axis_size("pipe")
    rep_count = lax.axis_size("rep")
    offset = lax.axis_index("tp") * local_width
    exponent = gossip_exp[0]
    levels = rep_count.bit_length() - 1
    choices = levels**pipe_count
    everyone = choices <= MOST_BRANCHES

    bwd_full = gathered(bwd_in[0, 0], 1)
    gain_full = gathered(gain_local, 0)
    fwd_other = shifted(fwd_rows, "tp", 1)
    width = bwd_full.shape[1]
    in_scale = width ** (-0.5)
    if everyone:
        place = jnp.int32(1)
        for p in range(1, pipe_count):
            place = jnp.where(lax.axis_index("pipe") >= p, place * levels, place)
        code = total_over(gossip_exp * place, "pipe")[0]

    scaled_b, inv_b, normed_b = normalize(bwd_full, gain_full)
    query_heads, keys, probs = attend(normed_b, seg_bwd[0, 0], query_weight, key_weight)
    scaled_own = lax.dynamic_slice_in_dim(scaled_b, offset, local_width, 1)
    value_heads = lax.dynamic_slice_in_dim(normed_b, offset, local_width, 1).reshape(count, heads, HEAD)
    grad_heads = grad_rows.reshape(count, heads, HEAD)
    value_grad = jnp.einsum("hrs,rhd->shd", probs, grad_heads, preferred_element_type=F32).reshape(
        count, local_width
    )
    prob_grad = jnp.einsum("rhd,shd->hrs", grad_heads, value_heads, preferred_element_type=F32)
    prob_f = probs.astype(F32)
    score_grad = (
        prob_f * (prob_grad - jnp.sum(prob_grad * prob_f, axis=-1, keepdims=True)) * HEAD ** (-0.5)
    ).astype(BF16)
    query_grad = (
        jnp.einsum("hrs,sd->rhd", score_grad, keys, preferred_element_type=F32)
        .reshape(count, local_width)
        .astype(BF16)
    )
    key_part = jnp.einsum("hrs,rhd->sd", score_grad, query_heads, preferred_element_type=F32)
    key_grad = (key_part + shifted(key_part.astype(BF16), "tp", 1).astype(F32)).astype(BF16)

    def rows_of(weight, start):
        return lax.dynamic_slice_in_dim(weight, start, local_width, 0)

    def through(grad, weight):
        return lax.dot_general(grad, weight, LAST, preferred_element_type=F32) * in_scale

    away = through(query_grad, rows_of(query_weight, width - local_width - offset)).astype(BF16)
    normed_grad = (
        through(query_grad, rows_of(query_weight, offset))
        + value_grad
        + shifted(away, "tp", 1).astype(F32)
        + through(key_grad, rows_of(key_weight, offset))
    )
    grad_gain = jnp.sum(normed_grad * scaled_own, axis=0)

    def gram(block):
        return lax.dot_general(block, block, LAST, preferred_element_type=F32)

    normed_gram = gram(normed_b)
    squares = (
        jnp.sum(normed_gram * (gram(query_grad) + gram(key_grad) / tp_count)) / width
        + jnp.sum(grad_gain * grad_gain)
    ).reshape(1, 1)
    squares = total_over(total_over(squares, "tp"), "pipe")[0, 0]
    inverse = lax.rsqrt(squares / (pipe_count * (width * width + width * HEAD + width)) + STEP_EPS)

    values = (fwd_rows, fwd_other, grad_rows, seg_fwd[0, 0], query_weight, key_weight, gain_local, gain_full)
    values += (normed_b, scaled_own, inv_b, query_grad, key_grad, normed_grad, grad_gain, inverse)
    if everyone:
        plans = []
        for number in range(choices):
            digits = [number // levels**p % levels for p in range(pipe_count)]
            plans.append(routes(digits, rep_count))
        branches = [partial(finish, plan=plan, along=True) for plan in plans]
        outs = lax.switch(code, branches, values)
    else:
        branches = [partial(finish, plan=straight(k, rep_count), along=False) for k in range(levels)]
        outs = list(lax.switch(exponent, branches, values))
        outs[0] = shifted(outs[0], "pipe", 1)
        outs[1] = shifted(outs[1], "pipe", -1)
    return tuple(out[None, None] for out in outs)


def solution(mesh):
    rows = P("rep", "pipe", None, "tp")
    tokens = P("rep", "pipe", None)
    keyed = P("rep", "pipe", None, None)
    line = P("rep", "pipe", "tp")
    return jax.shard_map(
        shards,
        mesh=mesh,
        in_specs=(rows, rows, rows, tokens, tokens, rows, keyed, line, P("pipe")),
        out_specs=(rows, rows, rows, keyed, line),
        check_vma=False,
    )
```

```python
from functools import partial

import jax
import jax.numpy as jnp
from jax import lax
from jax.experimental import pallas as pl
from jax.experimental.pallas import tpu as pltpu
from jax.sharding import PartitionSpec as P

HEAD = 128
LN_EPS = 1e-05
STEP_EPS = 1e-06
LEARN_RATE = 0.2
MASK_FILL = -1e30
CHUNK = 16
PIECES = 12
F32 = jnp.float32
BF16 = jnp.bfloat16
LAST = (((1,), (1,)), ((), ()))
FIRST = (((0,), (0,)), ((), ()))
VMEM_LIMIT = 48 * 1024 * 1024


def shifted(block, axis, by):
    length = lax.axis_size(axis)
    return lax.ppermute(block, axis, [(i, (i + by) % length) for i in range(length)])


def total_over(value, axis):
    parts = [shifted(value, axis, by) for by in range(1, lax.axis_size(axis))]
    for part in parts:
        value = value + part
    return value


def dot(a, b, dims=(((1,), (0,)), ((), ()))):
    return lax.dot_general(a, b, dims, preferred_element_type=F32)


def call(kernel, name, grid, prefetch, in_specs, out_specs, out_shape, scratch=(), cost=None):
    return pl.pallas_call(
        kernel,
        name=name,
        grid_spec=pltpu.PrefetchScalarGridSpec(
            num_scalar_prefetch=prefetch,
            grid=grid,
            in_specs=in_specs,
            out_specs=out_specs,
            scratch_shapes=list(scratch),
        ),
        out_shape=out_shape,
        cost_estimate=cost,
        compiler_params=pltpu.CompilerParams(vmem_limit_bytes=VMEM_LIMIT),
    )


def whole(shape):
    return pl.BlockSpec(shape, lambda *_: (0,) * len(shape))


def project_kernel(at, *refs):
    *batches, gain_own, gain_other, weight, key_weight, q, k, h, xhat, inv = refs
    count, local = xhat.shape
    width = 2 * local
    scale = width ** (-0.5)

    @pl.when(pl.program_id(0) == 0)
    def _():
        mine = pl.multiple_of(at[0] * local, HEAD)
        rest = pl.multiple_of((1 - at[0]) * local, HEAD)
        gain_a, gain_b = gain_own[...].astype(F32), gain_other[...].astype(F32)

        def some(batch, n):
            own, other = batches[2 * batch : 2 * batch + 2]
            rows = pl.ds(pl.multiple_of(n * CHUNK, CHUNK), CHUNK)
            a, b = own[rows, :].astype(F32), other[rows, :].astype(F32)
            mean = (jnp.sum(a, axis=1, keepdims=True) + jnp.sum(b, axis=1, keepdims=True)) / width
            a, b = a - mean, b - mean
            var = (jnp.sum(a * a, axis=1, keepdims=True) + jnp.sum(b * b, axis=1, keepdims=True)) / width
            inv_std = lax.rsqrt(var + LN_EPS)
            a, b = a * inv_std, b * inv_std
            to = pl.ds(pl.multiple_of(batch * count + n * CHUNK, CHUNK), CHUNK)
            h[to, pl.ds(mine, local)] = (a * gain_a).astype(BF16)
            h[to, pl.ds(rest, local)] = (b * gain_b).astype(BF16)
            if batch == 0:
                xhat[rows, :] = a
                inv[rows, :] = inv_std

        def both(n, carry):
            some(0, n)
            some(1, n)
            return carry

        lax.fori_loop(0, count // CHUNK, both, 0, unroll=2)
        k[...] = (dot(h[...], key_weight[...]) * scale).astype(BF16)

    q[...] = (dot(h[...], weight[...]) * scale).astype(BF16)


def project(at, batches, gain_own, gain_other, weight, key_weight):
    count, local = batches[0].shape
    width = 2 * local
    block = 256
    return call(
        project_kernel,
        "project",
        (weight.shape[1] // block,),
        1,
        [whole((count, local))] * 4
        + [
            whole((1, local)),
            whole((1, local)),
            pl.BlockSpec((width, block), lambda j, at: (0, j)),
            whole((width, HEAD)),
        ],
        [
            pl.BlockSpec((2 * count, block), lambda j, at: (0, j)),
            whole((2 * count, HEAD)),
            whole((2 * count, width)),
            whole((count, local)),
            whole((count, 1)),
        ],
        [
            jax.ShapeDtypeStruct((2 * count, weight.shape[1]), BF16),
            jax.ShapeDtypeStruct((2 * count, HEAD), BF16),
            jax.ShapeDtypeStruct((2 * count, width), BF16),
            jax.ShapeDtypeStruct((count, local), F32),
            jax.ShapeDtypeStruct((count, 1), F32),
        ],
        cost=pl.CostEstimate(
            flops=4 * count * width * local, bytes_accessed=2 * weight.size + 16 * count * local, transcendentals=0
        ),
    )(at, *batches, gain_own, gain_other, weight, key_weight)


def softmax(q, k, seg_col, seg_row):
    scores = dot(q, k, LAST) * HEAD ** (-0.5)
    scores = jnp.where(seg_col == seg_row, scores, MASK_FILL)
    expo = jnp.exp(scores - jnp.max(scores, axis=1, keepdims=True))
    return (expo / jnp.sum(expo, axis=1, keepdims=True)).astype(BF16)


def backward_kernel(at, q, k, v, g, seg_col, seg_row, dq, dv, dk):
    @pl.when(pl.program_id(0) == 0)
    def _():
        dk[...] = jnp.zeros_like(dk)

    keys = k[...]
    added = jnp.zeros(dk.shape, F32)
    for start in range(0, q.shape[1], HEAD):
        cols = slice(start, start + HEAD)
        probs = softmax(q[:, cols], keys, seg_col[...], seg_row[...])
        grads = g[:, cols]
        prob_grad = dot(grads, v[:, cols], LAST)
        prob_f = probs.astype(F32)
        inner = jnp.sum(prob_grad * prob_f, axis=1, keepdims=True)
        score_grad = (prob_f * (prob_grad - inner) * HEAD ** (-0.5)).astype(BF16)
        dv[:, cols] = dot(probs, grads, FIRST)
        dq[:, cols] = dot(score_grad, keys).astype(BF16)
        added = added + dot(score_grad, q[:, cols], FIRST)
    dk[...] += added


def heads_at(rows, start, block):
    if start:
        return pl.BlockSpec((rows, block), lambda j, at: (0, j + at[0] * start))
    return pl.BlockSpec((rows, block), lambda j, at: (0, j))


def attention_cost(count, local, products):
    heads = local // HEAD
    return pl.CostEstimate(
        flops=2 * products * heads * count * count * HEAD,
        bytes_accessed=10 * count * local,
        transcendentals=heads * count * count,
    )


def backward(at, q, k, normed, grads, seg, group=4):
    count, local = grads.shape
    block = group * HEAD
    half = local // block
    return call(
        backward_kernel,
        "backward",
        (half,),
        1,
        [
            heads_at(count, 0, block),
            whole((count, HEAD)),
            heads_at(count, half, block),
            heads_at(count, 0, block),
            whole((count, 1)),
            whole((1, count)),
        ],
        [heads_at(count, 0, block), heads_at(count, 0, block), whole((count, HEAD))],
        [
            jax.ShapeDtypeStruct((count, local), BF16),
            jax.ShapeDtypeStruct((count, local), F32),
            jax.ShapeDtypeStruct((count, HEAD), F32),
        ],
        cost=attention_cost(count, local, 5),
    )(at, q, k, normed, grads, seg.reshape(-1, 1), seg.reshape(1, -1))


def forward_kernel(at, q, k, v, x, seg_col, seg_row, y):
    keys = k[...]
    for start in range(0, q.shape[1], HEAD):
        cols = slice(start, start + HEAD)
        probs = softmax(q[:, cols], keys, seg_col[...], seg_row[...])
        y[:, cols] = (x[:, cols].astype(F32) + dot(probs, v[:, cols])).astype(BF16)


def forward(at, q, k, normed, rows, seg, group=6):
    count, local = rows.shape
    block = group * HEAD
    half = local // block
    return call(
        forward_kernel,
        "forward",
        (half,),
        1,
        [
            pl.BlockSpec((count, block), lambda j, at: (1, j)),
            pl.BlockSpec((count, HEAD), lambda j, at: (1, 0)),
            pl.BlockSpec((count, block), lambda j, at: (1, j + at[0] * half)),
            heads_at(count, 0, block),
            whole((count, 1)),
            whole((1, count)),
        ],
        heads_at(count, 0, block),
        jax.ShapeDtypeStruct((count, local), BF16),
        cost=attention_cost(count, local, 2),
    )(at, q, k, normed, rows, seg.reshape(-1, 1), seg.reshape(1, -1))


def away_kernel(at, dq, weight, out):
    out[...] = (dot(dq[...], weight[...], LAST) * (2 * dq.shape[1]) ** (-0.5)).astype(BF16)


def away(at, dq, weight, block=512):
    count, local = dq.shape
    half = local // block
    return call(
        away_kernel,
        "away",
        (half,),
        1,
        [whole((count, local)), pl.BlockSpec((block, local), lambda j, at: (j + (1 - at[0]) * half, 0))],
        pl.BlockSpec((count, block), lambda j, at: (0, j)),
        jax.ShapeDtypeStruct((count, local), BF16),
        cost=pl.CostEstimate(flops=2 * count * local * local, bytes_accessed=2 * local * local, transcendentals=0),
    )(at, dq, weight)


def home_kernel(at, dq, weight, dv, dk, key_weight, normed, out, gram):
    local = dq.shape[1]
    scale = (2 * local) ** (-0.5)
    out[...] = (dot(dq[...], weight[...], LAST) + dot(dk[...], key_weight[...], LAST)) * scale + dv[...]

    @pl.when(pl.program_id(0) == pl.num_programs(0) - 1)
    def _():
        rows = dot(normed[...], normed[...], LAST)
        steps = dot(dq[...], dq[...], LAST) + 0.5 * dot(dk[...], dk[...], LAST)
        part = jnp.sum(rows * steps, axis=0, keepdims=True)
        gram[...] = jnp.sum(part, axis=1, keepdims=True) / (2 * local)


def home(at, dq, weight, dv, dk, key_weight, normed, block=512):
    count, local = dq.shape
    half = local // block
    return call(
        home_kernel,
        "home",
        (half,),
        1,
        [
            whole((count, local)),
            pl.BlockSpec((block, local), lambda j, at: (j + at[0] * half, 0)),
            pl.BlockSpec((count, block), lambda j, at: (0, j)),
            whole((count, HEAD)),
            pl.BlockSpec((block, HEAD), lambda j, at: (j + at[0] * half, 0)),
            pl.BlockSpec((count, 2 * local), lambda j, at: (0, 0)),
        ],
        [pl.BlockSpec((count, block), lambda j, at: (0, j)), whole((1, 1))],
        [jax.ShapeDtypeStruct((count, local), F32), jax.ShapeDtypeStruct((1, 1), F32)],
        cost=pl.CostEstimate(flops=2 * count * local * local, bytes_accessed=2 * local * local, transcendentals=0),
    )(at, dq, weight, dv, dk, key_weight, normed)


def gather_kernel(part, theirs, xhat, gain, gram, weighted, sums, grad_gain, squares):
    @pl.when(pl.program_id(0) == 0)
    def _():
        sums[...] = jnp.zeros_like(sums)
        squares[...] = gram[...]

    grad = part[...] + theirs[...].astype(F32)
    scaled = xhat[...]
    along = jnp.sum(grad * scaled, axis=0, keepdims=True)
    grad_gain[...] = along
    squares[...] += jnp.sum(along * along, axis=1, keepdims=True)
    grad = grad * gain[...].astype(F32)
    weighted[...] = grad
    sums[:, 0:1] += jnp.sum(grad, axis=1, keepdims=True)
    sums[:, 1:2] += jnp.sum(grad * scaled, axis=1, keepdims=True)


def gather(part, theirs, xhat, gain, gram, block=512):
    count, local = part.shape
    wide = pl.BlockSpec((count, block), lambda j: (0, j))
    line = pl.BlockSpec((1, block), lambda j: (0, j))
    return call(
        gather_kernel,
        "gather",
        (local // block,),
        0,
        [wide, wide, wide, line, whole((1, 1))],
        [wide, whole((count, 2)), line, whole((1, 1))],
        [
            jax.ShapeDtypeStruct((count, local), F32),
            jax.ShapeDtypeStruct((count, 2), F32),
            jax.ShapeDtypeStruct((1, local), F32),
            jax.ShapeDtypeStruct((1, 1), F32),
        ],
        cost=pl.CostEstimate(flops=10 * count * local, bytes_accessed=18 * count * local, transcendentals=0),
    )(part, theirs, xhat, gain, gram)


def turn_kernel(weighted, xhat, inv, sums, others, grads, out):
    means = (sums[...] + others[...]) / (2 * xhat.shape[1])
    change = inv[...] * (weighted[...] - means[:, 0:1] - xhat[...] * means[:, 1:2])
    out[...] = (grads[...].astype(F32) + change).astype(BF16)


def turn(weighted, xhat, inv, sums, others, grads):
    count, local = grads.shape
    return call(
        turn_kernel,
        "turn",
        (1,),
        0,
        [whole((count, local)), whole((count, local)), whole((count, 1)), whole((count, 2)), whole((count, 2)), whole((count, local))],
        whole((count, local)),
        jax.ShapeDtypeStruct((count, local), BF16),
        cost=pl.CostEstimate(flops=6 * count * local, bytes_accessed=12 * count * local, transcendentals=0),
    )(weighted, xhat, inv, sums, others, grads)


def step_kernel(scale, normed, grads, weight, inverse, out):
    grad = dot(normed[...], grads[...], FIRST) * scale
    step = (LEARN_RATE * grad * inverse[...]).astype(BF16)
    out[...] = (weight[...].astype(F32) - step.astype(F32)).astype(BF16)


def step(normed, grads, weight, inverse, start, size):
    count, cols = grads.shape
    scale = weight.shape[0] ** (-0.5)
    block = min(size, 256)
    first = start // block
    return call(
        partial(step_kernel, scale),
        "step",
        (size // block,),
        0,
        [
            pl.BlockSpec((count, block), lambda j: (0, j + first)),
            whole((count, cols)),
            pl.BlockSpec((block, cols), lambda j: (j + first, 0)),
            whole((1, 1)),
        ],
        pl.BlockSpec((block, cols), lambda j: (j, 0)),
        jax.ShapeDtypeStruct((size, cols), BF16),
        cost=pl.CostEstimate(flops=2 * size * count * cols, bytes_accessed=4 * size * cols, transcendentals=0),
    )(normed, grads, weight, inverse)


def updated(weight, grad, inverse):
    change = (LEARN_RATE * grad * inverse).astype(BF16)
    return (weight.astype(F32) - change.astype(F32)).astype(BF16)


def small_kernel(at, normed, dk, key_weight, gain, grad_gain, inverse, out):
    local = normed.shape[1]
    grad = dot(normed[...], dk[...], FIRST) * (2 * local) ** (-0.5)
    out[:local, :] = updated(key_weight[...], grad, inverse[...])
    line = updated(gain[...], grad_gain[...], inverse[...]).astype(F32)
    rows = [line[:, s : s + HEAD] for s in range(0, local, HEAD)]
    rows.append(jnp.zeros((-len(rows) % 16, HEAD), F32))
    out[local:, :] = jnp.concatenate(rows, axis=0).astype(BF16)


def small_step(at, normed, dk, key_weight, gain, grad_gain, inverse):
    count = dk.shape[0]
    local = gain.shape[1]
    rows = local + -(-local // HEAD // 16) * 16
    return call(
        small_kernel,
        "small_step",
        (1,),
        1,
        [
            pl.BlockSpec((count, local), lambda j, at: (0, at[0])),
            whole((count, HEAD)),
            pl.BlockSpec((local, HEAD), lambda j, at: (at[0], 0)),
            whole((1, local)),
            whole((1, local)),
            whole((1, 1)),
        ],
        whole((rows, HEAD)),
        jax.ShapeDtypeStruct((rows, HEAD), BF16),
        cost=pl.CostEstimate(flops=2 * count * local * HEAD, bytes_accessed=2 * count * local, transcendentals=0),
    )(at, normed, dk, key_weight, gain, grad_gain, inverse)


def halves(mine, theirs):
    return ((mine.astype(F32) + theirs.astype(F32)) * 0.5).astype(BF16)


def halves_kernel(mine, theirs, *rest):
    rest[-1][...] = halves(mine[...], theirs[...])


def halves_into(whole_out, mine, theirs, start, rows):
    size, cols = mine.shape
    block = min(size, 128)
    first = start // block
    part = pl.BlockSpec((block, cols), lambda j: (j, 0))
    earlier = [] if whole_out is None else [whole_out]
    return pl.pallas_call(
        halves_kernel,
        name="halves",
        grid=(size // block,),
        in_specs=[part, part] + [pl.BlockSpec(memory_space=pl.ANY)] * len(earlier),
        out_specs=pl.BlockSpec((block, cols), lambda j: (j + first, 0)),
        out_shape=jax.ShapeDtypeStruct((rows, cols), BF16),
        input_output_aliases={2: 0} if earlier else {},
        cost_estimate=pl.CostEstimate(flops=2 * size * cols, bytes_accessed=6 * size * cols, transcendentals=0),
    )(mine, theirs, *earlier)


def column(p, level, rep_count, pipe_count):
    return [
        (r * pipe_count + p, (r ^ 1 << level) * pipe_count + p) for r in range(rep_count) if r ^ 1 << level < rep_count
    ]


def traded(mask, pipe_count):
    return [
        (r * pipe_count + p, r * pipe_count + (p ^ mask if r in (1, 2) else p)) for r in range(4) for p in range(pipe_count)
    ]


def sent(exponents, mask, pipe_count):
    hops = []
    for p, k in enumerate(exponents):
        q = p ^ mask
        hops += [(r * pipe_count + p, (r ^ 1 << k) * pipe_count + p) for r in (0, 3)]
        hops += [(r * pipe_count + p, (r ^ 1 << exponents[q]) * pipe_count + q) for r in (1, 2)]
    return hops


def straight(level, rep_count, pipe_count):
    return [(None, [hop for p in range(pipe_count) for hop in column(p, level, rep_count, pipe_count)])]


def crossed(bit, far_bit, pipe_count):
    exponents = [int(p >> bit & 1 == far_bit) for p in range(pipe_count)]
    return [(traded(1 << bit, pipe_count), sent(exponents, 1 << bit, pipe_count))]


def in_turn(near, pipe_count):
    exponents = [int(p != near) for p in range(pipe_count)]
    return [(traded(mask, pipe_count), sent(exponents, mask, pipe_count)) for mask in range(1, pipe_count)]


def choices(exponents):
    count = len(exponents)
    if sum(exponents) == count - 1:
        return [6 + exponents.index(0)] * count
    best = None
    for axes in range(1 << count):
        taken, pairs = list(exponents), 0
        for p, k in enumerate(exponents):
            bit = axes >> p & 1
            other = p ^ 1 << bit
            if axes >> other & 1 == bit and exponents[other] != k:
                far = p if k == 1 else other
                taken[p] = 2 + 2 * bit + (far >> bit & 1)
                pairs += 1
        if best is None or pairs > best[0]:
            best = (pairs, taken)
    return best[1]


def exchanged(chains, plan, token, take):
    axes = ("rep", "pipe")
    moved, landed, last, merged = [None, None], [None, None], [None, None], None
    made = [[], []]
    for at in range(max(len(blocks) for blocks in chains) + 1):
        for c, blocks in enumerate(chains):
            if at > len(blocks):
                continue
            hops = [plan[n % len(plan)] for n in (2 * at + c - 2, 2 * at + c)]
            going = None
            if at < len(blocks):
                made[c].append(blocks[at](token))
                going = made[c][-1]
            ready = last[c]
            tied = merged if at > 3 else None
            parts = [going, moved[c], landed[c], last[1 - c], tied, token if (at, c) == (1, 1) else None]
            held = iter(lax.optimization_barrier([part for part in parts if part is not None]))
            going, moved[c], landed[c], last[1 - c], tied, later = [None if part is None else next(held) for part in parts]
            token = token if later is None else later
            merged = merged if tied is None else tied
            if ready is not None:
                merged = take(merged, c, at - 3, made[c][at - 3], ready)
            last[c] = landed[c]
            landed[c] = None if moved[c] is None else lax.ppermute(moved[c], axes, hops[0][1])
            if going is not None and hops[1][0] is not None:
                going = lax.ppermute(going, axes, hops[1][0])
            moved[c] = going
    for c, blocks in enumerate(chains):
        merged = take(merged, c, len(blocks) - 2, made[c][-2], last[c])
        merged = take(merged, c, len(blocks) - 1, made[c][-1], landed[c])
    return merged


def swap(values, plan):
    at, early, normed, dq, query_weight, dk, key_weight, gain_own, grad_gain, inverse = values
    count, local = dq.shape
    width = 2 * local
    piece = early.shape[0] // 2
    split = 4 * piece
    made = {}

    def stepped(start, size):
        def make(token):
            low, high = (0, 2 * piece) if start < 2 * piece else (2 * piece, split) if start < split else (split, width)
            if low not in made:
                made[low] = step(normed, dq, query_weight, token, low, high - low) if low else early
            return lax.slice_in_dim(made[low], start - low, start - low + size, axis=0)

        return make

    evens = [(0, piece // 2)] + [(s, piece) for s in range(2 * piece, width, 2 * piece)] + [(piece // 2, piece // 2)]
    odds = [(s, piece) for s in range(piece, width, 2 * piece)]
    chains = [[stepped(*spot) for spot in spots] for spots in (evens, odds)]
    odds.insert(2, None)
    chains[1].insert(2, lambda token: small_step(at, normed, dk, key_weight, gain_own, grad_gain, token))
    small_out = []

    def take(merged, c, n, block, received):
        spot = (evens, odds)[c][n]
        if spot is None:
            small_out.append(halves(block, received))
            return merged
        return halves_into(merged, block, received, spot[0], width)

    merged = exchanged(chains, plan, inverse, take)
    small_out = small_out[0]
    mine = small_out[:local]
    theirs = shifted(mine, "tp", 1)
    key_out = jnp.where(
        at[0] == 0, jnp.concatenate([mine, theirs], axis=0), jnp.concatenate([theirs, mine], axis=0)
    )
    gain_out = small_out[local : local + local // HEAD].reshape(-1)
    return merged, key_out, gain_out


def shards(fwd_in, bwd_in, bwd_grad, seg_fwd, seg_bwd, w_query, w_key, gain, gossip_exp):
    query_weight = w_query[0, 0]
    key_weight = w_key[0, 0]
    gain_own = gain[0, 0].reshape(1, -1)
    grad_rows = bwd_grad[0, 0]
    count, local = grad_rows.shape
    width = 2 * local
    pipe_count = lax.axis_size("pipe")
    rep_count = lax.axis_size("rep")
    levels = rep_count.bit_length() - 1
    at = lax.axis_index("tp").astype(jnp.int32).reshape(1)
    exponent = gossip_exp[0]

    bwd_other = shifted(bwd_in[0, 0], "tp", 1)
    gain_other = shifted(gain_own, "tp", 1)
    gain_other, fwd_rows = lax.optimization_barrier((gain_other, fwd_in[0, 0]))
    fwd_other = shifted(fwd_rows, "tp", 1)

    q, k, normed, xhat, inv = project(
        at, (bwd_in[0, 0], bwd_other, fwd_in[0, 0], fwd_other), gain_own, gain_other, query_weight, key_weight
    )
    section_out = forward(at, q, k, normed, fwd_in[0, 0], seg_fwd[0, 0])
    q, section_out = lax.optimization_barrier((q, section_out))
    first_rows = shifted(section_out[: count // 2], "pipe", 1)
    dq, dv, key_part = backward(at, q, k, normed, grad_rows, seg_bwd[0, 0])
    dq, first_rows, section_out = lax.optimization_barrier((dq, first_rows, section_out))
    last_rows = shifted(section_out[count // 2 :], "pipe", 1)
    key_other = shifted(key_part.astype(BF16), "tp", 1)
    inward = shifted(away(at, dq, query_weight), "tp", 1)
    dk = (key_part + key_other.astype(F32)).astype(BF16)
    part, gram = home(at, dq, query_weight, dv, dk, key_weight, normed)
    weighted, sums, grad_gain, squares = gather(part, inward, xhat, gain_own, gram)
    last_rows, squares = lax.optimization_barrier((last_rows, squares))
    next_rows = jnp.concatenate([first_rows, last_rows], axis=0)
    squares = total_over(squares, "tp")

    bit = jnp.left_shift(gossip_exp, lax.axis_index("pipe").astype(jnp.int32)).astype(F32)
    totals = total_over(jnp.concatenate([squares, bit.reshape(1, 1)], axis=1), "pipe")
    total = pipe_count * (width * width + width * HEAD + width)
    inverse = lax.rsqrt(totals[:, 0:1] / total + STEP_EPS)
    plans = [straight(k, rep_count, pipe_count) for k in range(levels)]
    if rep_count == 4 and pipe_count == 4:
        plans += [crossed(bit, far, pipe_count) for bit in range(2) for far in range(2)]
        plans += [in_turn(p, pipe_count) for p in range(pipe_count)]
        table = [choices([n >> p & 1 for p in range(pipe_count)]) for n in range(1 << pipe_count)]
        own = jnp.asarray(table, jnp.int32)
        place = totals[0, 1].astype(jnp.int32) * pipe_count + lax.axis_index("pipe")
        exponent = jnp.sum(jnp.where(jnp.arange(own.size) == place, own.reshape(-1), 0))

    back_rows = turn(weighted, xhat, inv, sums, shifted(sums, "tp", 1), grad_rows)
    back_rows, inverse = lax.optimization_barrier((back_rows, inverse))
    prev_rows = shifted(back_rows, "pipe", -1)
    early = step(normed, dq, query_weight, inverse, 0, 2 * width // PIECES)
    values = (at, early, normed, dq, query_weight, dk, key_weight, gain_own, grad_gain, inverse)
    query_out, key_out, gain_out = lax.switch(exponent, [partial(swap, plan=plan) for plan in plans], values)
    outs = (next_rows, prev_rows, query_out, key_out, gain_out)
    return tuple(out[None, None] for out in outs)


def solution(mesh):
    rows = P("rep", "pipe", None, "tp")
    tokens = P("rep", "pipe", None)
    keyed = P("rep", "pipe", None, None)
    line = P("rep", "pipe", "tp")
    return jax.shard_map(
        shards,
        mesh=mesh,
        in_specs=(rows, rows, rows, tokens, tokens, rows, keyed, line, P("pipe")),
        out_specs=(rows, rows, rows, keyed, line),
        check_vma=False,
    )
```

```python
from functools import partial

import jax
import jax.numpy as jnp
from jax import lax
from jax.experimental import pallas as pl
from jax.experimental.pallas import tpu as pltpu
from jax.sharding import PartitionSpec as P

HEAD = 128
LN_EPS = 1e-05
STEP_EPS = 1e-06
LEARN_RATE = 0.2
MASK_FILL = -1e30
CHUNK = 16
PIECES = 12
F32 = jnp.float32
BF16 = jnp.bfloat16
LAST = (((1,), (1,)), ((), ()))
FIRST = (((0,), (0,)), ((), ()))
VMEM_LIMIT = 48 * 1024 * 1024


def shifted(block, axis, by):
    length = lax.axis_size(axis)
    return lax.ppermute(block, axis, [(i, (i + by) % length) for i in range(length)])


def total_over(value, axis):
    parts = [shifted(value, axis, by) for by in range(1, lax.axis_size(axis))]
    for part in parts:
        value = value + part
    return value


def dot(a, b, dims=(((1,), (0,)), ((), ()))):
    return lax.dot_general(a, b, dims, preferred_element_type=F32)


def call(kernel, name, grid, prefetch, in_specs, out_specs, out_shape, scratch=(), cost=None):
    return pl.pallas_call(
        kernel,
        name=name,
        grid_spec=pltpu.PrefetchScalarGridSpec(
            num_scalar_prefetch=prefetch,
            grid=grid,
            in_specs=in_specs,
            out_specs=out_specs,
            scratch_shapes=list(scratch),
        ),
        out_shape=out_shape,
        cost_estimate=cost,
        compiler_params=pltpu.CompilerParams(vmem_limit_bytes=VMEM_LIMIT),
    )


def whole(shape):
    return pl.BlockSpec(shape, lambda *_: (0,) * len(shape))


def project_kernel(at, *refs):
    *arrays, gain_own, gain_other, q, k, h, xhat, inv, rows, key_rows, blocks, arrived = refs
    *batches, weight, key_weight = arrays
    count, local = xhat.shape
    width = 2 * local
    scale = width ** (-0.5)
    block = blocks.shape[2]

    def block_copy(j):
        columns = pl.ds(pl.multiple_of(j * block, block), block)
        return pltpu.make_async_copy(weight.at[:, columns], blocks.at[j], arrived.at[len(batches) + 1 + j])

    copies = [pltpu.make_async_copy(ref, rows.at[i], arrived.at[i]) for i, ref in enumerate(batches)]
    copies.append(pltpu.make_async_copy(key_weight, key_rows, arrived.at[len(batches)]))
    for copy in copies:
        copy.start()
    for j in range(blocks.shape[0]):
        block_copy(j).start()

    mine = pl.multiple_of(at[0] * local, HEAD)
    rest = pl.multiple_of((1 - at[0]) * local, HEAD)
    gain_a, gain_b = gain_own[...].astype(F32), gain_other[...].astype(F32)
    for batch in range(2):
        copies[2 * batch].wait()
        copies[2 * batch + 1].wait()

        def some(n, carry):
            part = pl.ds(pl.multiple_of(n * CHUNK, CHUNK), CHUNK)
            a, b = rows[2 * batch, part, :].astype(F32), rows[2 * batch + 1, part, :].astype(F32)
            mean = (jnp.sum(a, axis=1, keepdims=True) + jnp.sum(b, axis=1, keepdims=True)) / width
            a, b = a - mean, b - mean
            var = (jnp.sum(a * a, axis=1, keepdims=True) + jnp.sum(b * b, axis=1, keepdims=True)) / width
            inv_std = lax.rsqrt(var + LN_EPS)
            a, b = a * inv_std, b * inv_std
            to = pl.ds(pl.multiple_of(batch * count + n * CHUNK, CHUNK), CHUNK)
            h[to, pl.ds(mine, local)] = (a * gain_a).astype(BF16)
            h[to, pl.ds(rest, local)] = (b * gain_b).astype(BF16)
            if batch == 0:
                xhat[part, :] = a
                inv[part, :] = inv_std
            return carry

        lax.fori_loop(0, count // CHUNK, some, 0, unroll=4)

    copies[-1].wait()
    k[...] = (dot(h[...], key_rows[...]) * scale).astype(BF16)

    def one(j, carry):
        block_copy(j).wait()
        q[:, pl.ds(pl.multiple_of(j * block, block), block)] = (dot(h[...], blocks[j]) * scale).astype(BF16)
        return carry

    lax.fori_loop(0, blocks.shape[0], one, 0)


def project(at, batches, gain_own, gain_other, weight, key_weight):
    count, local = batches[0].shape
    width = 2 * local
    block = 256
    parts = weight.shape[1] // block
    shapes = [
        jax.ShapeDtypeStruct((2 * count, weight.shape[1]), BF16),
        jax.ShapeDtypeStruct((2 * count, HEAD), BF16),
        jax.ShapeDtypeStruct((2 * count, width), BF16),
        jax.ShapeDtypeStruct((count, local), F32),
        jax.ShapeDtypeStruct((count, 1), F32),
    ]
    return call(
        project_kernel,
        "project",
        (1,),
        1,
        [pl.BlockSpec(memory_space=pl.ANY)] * 6 + [whole((1, local))] * 2,
        [whole(s.shape) for s in shapes],
        shapes,
        scratch=[
            pltpu.VMEM((4, count, local), BF16),
            pltpu.VMEM((width, HEAD), BF16),
            pltpu.VMEM((parts, width, block), BF16),
            pltpu.SemaphoreType.DMA((5 + parts,)),
        ],
        cost=pl.CostEstimate(
            flops=4 * count * width * local, bytes_accessed=2 * weight.size + 16 * count * local, transcendentals=0
        ),
    )(at, *batches, weight, key_weight, gain_own, gain_other)


def softmax(q, k, seg_col, seg_row):
    scores = dot(q, k, LAST) * HEAD ** (-0.5)
    scores = jnp.where(seg_col == seg_row, scores, MASK_FILL)
    expo = jnp.exp(scores - jnp.max(scores, axis=1, keepdims=True))
    return (expo / jnp.sum(expo, axis=1, keepdims=True)).astype(BF16)


def backward_kernel(at, q, k, v, g, seg_col, seg_row, dq, dv, dk):
    @pl.when(pl.program_id(0) == 0)
    def _():
        dk[...] = jnp.zeros_like(dk)

    keys = k[...]
    added = jnp.zeros(dk.shape, F32)
    for start in range(0, q.shape[1], HEAD):
        cols = slice(start, start + HEAD)
        probs = softmax(q[:, cols], keys, seg_col[...], seg_row[...])
        grads = g[:, cols]
        prob_grad = dot(grads, v[:, cols], LAST)
        prob_f = probs.astype(F32)
        inner = jnp.sum(prob_grad * prob_f, axis=1, keepdims=True)
        score_grad = (prob_f * (prob_grad - inner) * HEAD ** (-0.5)).astype(BF16)
        dv[:, cols] = dot(probs, grads, FIRST)
        dq[:, cols] = dot(score_grad, keys).astype(BF16)
        added = added + dot(score_grad, q[:, cols], FIRST)
    dk[...] += added


def heads_at(rows, start, block):
    if start:
        return pl.BlockSpec((rows, block), lambda j, at: (0, j + at[0] * start))
    return pl.BlockSpec((rows, block), lambda j, at: (0, j))


def attention_cost(count, local, products):
    heads = local // HEAD
    return pl.CostEstimate(
        flops=2 * products * heads * count * count * HEAD,
        bytes_accessed=10 * count * local,
        transcendentals=heads * count * count,
    )


def backward(at, q, k, normed, grads, seg, group=4):
    count, local = grads.shape
    block = group * HEAD
    half = local // block
    return call(
        backward_kernel,
        "backward",
        (half,),
        1,
        [
            heads_at(count, 0, block),
            whole((count, HEAD)),
            heads_at(count, half, block),
            heads_at(count, 0, block),
            whole((count, 1)),
            whole((1, count)),
        ],
        [heads_at(count, 0, block), heads_at(count, 0, block), whole((count, HEAD))],
        [
            jax.ShapeDtypeStruct((count, local), BF16),
            jax.ShapeDtypeStruct((count, local), F32),
            jax.ShapeDtypeStruct((count, HEAD), F32),
        ],
        cost=attention_cost(count, local, 5),
    )(at, q, k, normed, grads, seg.reshape(-1, 1), seg.reshape(1, -1))


def forward_kernel(at, q, k, v, x, seg_col, seg_row, y):
    keys = k[...]
    for start in range(0, q.shape[1], HEAD):
        cols = slice(start, start + HEAD)
        probs = softmax(q[:, cols], keys, seg_col[...], seg_row[...])
        y[:, cols] = (x[:, cols].astype(F32) + dot(probs, v[:, cols])).astype(BF16)


def forward(at, q, k, normed, rows, seg, group=6):
    count, local = rows.shape
    block = group * HEAD
    half = local // block
    return call(
        forward_kernel,
        "forward",
        (half,),
        1,
        [
            pl.BlockSpec((count, block), lambda j, at: (1, j)),
            pl.BlockSpec((count, HEAD), lambda j, at: (1, 0)),
            pl.BlockSpec((count, block), lambda j, at: (1, j + at[0] * half)),
            heads_at(count, 0, block),
            whole((count, 1)),
            whole((1, count)),
        ],
        heads_at(count, 0, block),
        jax.ShapeDtypeStruct((count, local), BF16),
        cost=attention_cost(count, local, 2),
    )(at, q, k, normed, rows, seg.reshape(-1, 1), seg.reshape(1, -1))


def away_kernel(at, dq, weight, out):
    out[...] = (dot(dq[...], weight[...], LAST) * (2 * dq.shape[1]) ** (-0.5)).astype(BF16)


def away(at, dq, weight, block=512):
    count, local = dq.shape
    half = local // block
    return call(
        away_kernel,
        "away",
        (half,),
        1,
        [whole((count, local)), pl.BlockSpec((block, local), lambda j, at: (j + (1 - at[0]) * half, 0))],
        pl.BlockSpec((count, block), lambda j, at: (0, j)),
        jax.ShapeDtypeStruct((count, local), BF16),
        cost=pl.CostEstimate(flops=2 * count * local * local, bytes_accessed=2 * local * local, transcendentals=0),
    )(at, dq, weight)


def home_kernel(at, dq, weight, dv, dk, key_weight, normed, out, gram):
    local = dq.shape[1]
    scale = (2 * local) ** (-0.5)
    out[...] = (dot(dq[...], weight[...], LAST) + dot(dk[...], key_weight[...], LAST)) * scale + dv[...]

    @pl.when(pl.program_id(0) == pl.num_programs(0) - 1)
    def _():
        rows = dot(normed[...], normed[...], LAST)
        steps = dot(dq[...], dq[...], LAST) + 0.5 * dot(dk[...], dk[...], LAST)
        part = jnp.sum(rows * steps, axis=0, keepdims=True)
        gram[...] = jnp.sum(part, axis=1, keepdims=True) / (2 * local)


def home(at, dq, weight, dv, dk, key_weight, normed, block=512):
    count, local = dq.shape
    half = local // block
    return call(
        home_kernel,
        "home",
        (half,),
        1,
        [
            whole((count, local)),
            pl.BlockSpec((block, local), lambda j, at: (j + at[0] * half, 0)),
            pl.BlockSpec((count, block), lambda j, at: (0, j)),
            whole((count, HEAD)),
            pl.BlockSpec((block, HEAD), lambda j, at: (j + at[0] * half, 0)),
            pl.BlockSpec((count, 2 * local), lambda j, at: (0, 0)),
        ],
        [pl.BlockSpec((count, block), lambda j, at: (0, j)), whole((1, 1))],
        [jax.ShapeDtypeStruct((count, local), F32), jax.ShapeDtypeStruct((1, 1), F32)],
        cost=pl.CostEstimate(flops=2 * count * local * local, bytes_accessed=2 * local * local, transcendentals=0),
    )(at, dq, weight, dv, dk, key_weight, normed)


def gather_kernel(part, theirs, xhat, gain, gram, weighted, sums, grad_gain, squares):
    @pl.when(pl.program_id(0) == 0)
    def _():
        sums[...] = jnp.zeros_like(sums)
        squares[...] = gram[...]

    grad = part[...] + theirs[...].astype(F32)
    scaled = xhat[...]
    along = jnp.sum(grad * scaled, axis=0, keepdims=True)
    grad_gain[...] = along
    squares[...] += jnp.sum(along * along, axis=1, keepdims=True)
    grad = grad * gain[...].astype(F32)
    weighted[...] = grad
    sums[:, 0:1] += jnp.sum(grad, axis=1, keepdims=True)
    sums[:, 1:2] += jnp.sum(grad * scaled, axis=1, keepdims=True)


def gather(part, theirs, xhat, gain, gram, block=512):
    count, local = part.shape
    wide = pl.BlockSpec((count, block), lambda j: (0, j))
    line = pl.BlockSpec((1, block), lambda j: (0, j))
    return call(
        gather_kernel,
        "gather",
        (local // block,),
        0,
        [wide, wide, wide, line, whole((1, 1))],
        [wide, whole((count, 2)), line, whole((1, 1))],
        [
            jax.ShapeDtypeStruct((count, local), F32),
            jax.ShapeDtypeStruct((count, 2), F32),
            jax.ShapeDtypeStruct((1, local), F32),
            jax.ShapeDtypeStruct((1, 1), F32),
        ],
        cost=pl.CostEstimate(flops=10 * count * local, bytes_accessed=18 * count * local, transcendentals=0),
    )(part, theirs, xhat, gain, gram)


def turn_kernel(weighted, xhat, inv, sums, others, grads, out):
    means = (sums[...] + others[...]) / (2 * xhat.shape[1])
    change = inv[...] * (weighted[...] - means[:, 0:1] - xhat[...] * means[:, 1:2])
    out[...] = (grads[...].astype(F32) + change).astype(BF16)


def turn(weighted, xhat, inv, sums, others, grads):
    count, local = grads.shape
    return call(
        turn_kernel,
        "turn",
        (1,),
        0,
        [whole((count, local)), whole((count, local)), whole((count, 1)), whole((count, 2)), whole((count, 2)), whole((count, local))],
        whole((count, local)),
        jax.ShapeDtypeStruct((count, local), BF16),
        cost=pl.CostEstimate(flops=6 * count * local, bytes_accessed=12 * count * local, transcendentals=0),
    )(weighted, xhat, inv, sums, others, grads)


def step_kernel(scale, normed, grads, weight, inverse, out):
    grad = dot(normed[...], grads[...], FIRST) * scale
    step = (LEARN_RATE * grad * inverse[...]).astype(BF16)
    out[...] = (weight[...].astype(F32) - step.astype(F32)).astype(BF16)


def step(normed, grads, weight, inverse, start, size):
    count, cols = grads.shape
    scale = weight.shape[0] ** (-0.5)
    block = min(size, 256)
    first = start // block
    return call(
        partial(step_kernel, scale),
        "step",
        (size // block,),
        0,
        [
            pl.BlockSpec((count, block), lambda j: (0, j + first)),
            whole((count, cols)),
            pl.BlockSpec((block, cols), lambda j: (j + first, 0)),
            whole((1, 1)),
        ],
        pl.BlockSpec((block, cols), lambda j: (j, 0)),
        jax.ShapeDtypeStruct((size, cols), BF16),
        cost=pl.CostEstimate(flops=2 * size * count * cols, bytes_accessed=4 * size * cols, transcendentals=0),
    )(normed, grads, weight, inverse)


def updated(weight, grad, inverse):
    change = (LEARN_RATE * grad * inverse).astype(BF16)
    return (weight.astype(F32) - change.astype(F32)).astype(BF16)


def small_kernel(at, normed, dk, key_weight, gain, grad_gain, inverse, out):
    local = normed.shape[1]
    grad = dot(normed[...], dk[...], FIRST) * (2 * local) ** (-0.5)
    out[:local, :] = updated(key_weight[...], grad, inverse[...])
    line = updated(gain[...], grad_gain[...], inverse[...]).astype(F32)
    rows = [line[:, s : s + HEAD] for s in range(0, local, HEAD)]
    rows.append(jnp.zeros((-len(rows) % 16, HEAD), F32))
    out[local:, :] = jnp.concatenate(rows, axis=0).astype(BF16)


def small_step(at, normed, dk, key_weight, gain, grad_gain, inverse):
    count = dk.shape[0]
    local = gain.shape[1]
    rows = local + -(-local // HEAD // 16) * 16
    return call(
        small_kernel,
        "small_step",
        (1,),
        1,
        [
            pl.BlockSpec((count, local), lambda j, at: (0, at[0])),
            whole((count, HEAD)),
            pl.BlockSpec((local, HEAD), lambda j, at: (at[0], 0)),
            whole((1, local)),
            whole((1, local)),
            whole((1, 1)),
        ],
        whole((rows, HEAD)),
        jax.ShapeDtypeStruct((rows, HEAD), BF16),
        cost=pl.CostEstimate(flops=2 * count * local * HEAD, bytes_accessed=2 * count * local, transcendentals=0),
    )(at, normed, dk, key_weight, gain, grad_gain, inverse)


def halves(mine, theirs):
    return ((mine.astype(F32) + theirs.astype(F32)) * 0.5).astype(BF16)


def halves_kernel(mine, theirs, *rest):
    rest[-1][...] = halves(mine[...], theirs[...])


def halves_into(whole_out, mine, theirs, start, rows):
    size, cols = mine.shape
    block = min(size, 128)
    first = start // block
    part = pl.BlockSpec((block, cols), lambda j: (j, 0))
    earlier = [] if whole_out is None else [whole_out]
    return pl.pallas_call(
        halves_kernel,
        name="halves",
        grid=(size // block,),
        in_specs=[part, part] + [pl.BlockSpec(memory_space=pl.ANY)] * len(earlier),
        out_specs=pl.BlockSpec((block, cols), lambda j: (j + first, 0)),
        out_shape=jax.ShapeDtypeStruct((rows, cols), BF16),
        input_output_aliases={2: 0} if earlier else {},
        cost_estimate=pl.CostEstimate(flops=2 * size * cols, bytes_accessed=6 * size * cols, transcendentals=0),
    )(mine, theirs, *earlier)


def column(p, level, rep_count, pipe_count):
    return [
        (r * pipe_count + p, (r ^ 1 << level) * pipe_count + p) for r in range(rep_count) if r ^ 1 << level < rep_count
    ]


def traded(mask, pipe_count):
    return [
        (r * pipe_count + p, r * pipe_count + (p ^ mask if r in (1, 2) else p)) for r in range(4) for p in range(pipe_count)
    ]


def sent(exponents, mask, pipe_count):
    hops = []
    for p, k in enumerate(exponents):
        q = p ^ mask
        hops += [(r * pipe_count + p, (r ^ 1 << k) * pipe_count + p) for r in (0, 3)]
        hops += [(r * pipe_count + p, (r ^ 1 << exponents[q]) * pipe_count + q) for r in (1, 2)]
    return hops


def straight(level, rep_count, pipe_count):
    send = [hop for p in range(pipe_count) for hop in column(p, level, rep_count, pipe_count)]
    return send, None, send


def crossed(bit, far_bit, rep_count, pipe_count):
    exponents = [int(p >> bit & 1 == far_bit) for p in range(pipe_count)]
    direct = [hop for p, k in enumerate(exponents) for hop in column(p, k, rep_count, pipe_count)]
    return direct, traded(1 << bit, pipe_count), sent(exponents, 1 << bit, pipe_count)


def choices(exponents):
    count = len(exponents)
    best = None
    for axes in range(1 << count):
        taken, pairs = list(exponents), 0
        for p, k in enumerate(exponents):
            bit = axes >> p & 1
            other = p ^ 1 << bit
            if axes >> other & 1 == bit and exponents[other] != k:
                far = p if k == 1 else other
                taken[p] = 2 + 2 * bit + (far >> bit & 1)
                pairs += 1
        if best is None or pairs > best[0]:
            best = (pairs, taken)
    return best[1]


def exchanged(first, chains, plan, token, take):
    axes = ("rep", "pipe")
    direct, trade, send = plan
    moved, landed, last, merged = [None, None], [None, None], [None, None], None
    made = [[], []]
    received = lax.ppermute(first, axes, direct)
    for at in range(max(len(blocks) for blocks in chains) + 1):
        for c, blocks in enumerate(chains):
            if at > len(blocks):
                continue
            going = None
            if at < len(blocks):
                made[c].append(blocks[at](token))
                going = made[c][-1]
            tied = merged if at > 3 else None
            parts = [going, moved[c], landed[c], last[1 - c], tied]
            parts += [token if (at, c) == (1, 1) else None, received if (at, c) == (1, 0) else None]
            held = iter(lax.optimization_barrier([part for part in parts if part is not None]))
            parts = [None if part is None else next(held) for part in parts]
            going, moved[c], landed[c], ready = parts[:4]
            merged, token, received = [a if b is None else b for a, b in zip((merged, token, received), parts[4:])]
            if (at, c) == (1, 0):
                merged = take(merged, None, None, first, received)
            if ready is not None:
                number = at - 3 + c
                merged = take(merged, 1 - c, number, made[1 - c][number], ready)
            last[1 - c], last[c] = None, landed[c]
            landed[c] = None if moved[c] is None else lax.ppermute(moved[c], axes, send)
            if going is not None and trade is not None:
                going = lax.ppermute(going, axes, trade)
            moved[c] = going
    for c, blocks in enumerate(chains):
        if last[c] is not None:
            merged = take(merged, c, len(blocks) - 2, made[c][-2], last[c])
        merged = take(merged, c, len(blocks) - 1, made[c][-1], landed[c])
    return merged


def swap(values, plan):
    at, early, normed, dq, query_weight, dk, key_weight, gain_own, grad_gain, inverse, *next_rows = values
    count, local = dq.shape
    width = 2 * local
    piece = early.shape[0] // 2
    split = 4 * piece
    made = {}

    def stepped(start, size):
        def make(token):
            low, high = (0, 2 * piece) if start < 2 * piece else (2 * piece, split) if start < split else (split, width)
            if low not in made:
                made[low] = step(normed, dq, query_weight, token, low, high - low) if low else early
            return lax.slice_in_dim(made[low], start - low, start - low + size, axis=0)

        return make

    short = piece // 2
    if plan[1] is None:
        evens = [(short, short)] + [(s, 2 * piece) for s in range(2 * piece, width, 4 * piece)]
        odds = [(piece, piece)] + [(s, 2 * piece) for s in range(4 * piece, width, 4 * piece)]
        odds.insert(-1, None)
    else:
        end = width - piece
        evens = [(short, short)] + [(s, piece) for s in range(2 * piece, end, 2 * piece)] + [(end + short, short)]
        odds = [(s, piece) for s in range(piece, end, 2 * piece)] + [None, (end, short)]
    chains = [
        [
            stepped(*spot)
            if spot
            else lambda token: small_step(at, normed, dk, key_weight, gain_own, grad_gain, token)
            for spot in spots
        ]
        for spots in (evens, odds)
    ]
    small_out = []

    def take(merged, c, n, block, received):
        spot = (0, short) if c is None else (evens, odds)[c][n]
        if spot is None:
            small_out.append(halves(block, received))
            return merged
        return halves_into(merged, block, received, spot[0], width)

    merged = exchanged(lax.slice_in_dim(early, 0, short, axis=0), chains, plan, inverse, take)
    small_out = small_out[0]
    mine = small_out[:local]
    theirs = shifted(mine, "tp", 1)
    key_out = jnp.where(
        at[0] == 0, jnp.concatenate([mine, theirs], axis=0), jnp.concatenate([theirs, mine], axis=0)
    )
    gain_out = small_out[local : local + local // HEAD].reshape(-1)
    return merged, key_out, gain_out, jnp.concatenate(next_rows, axis=0)


def shards(fwd_in, bwd_in, bwd_grad, seg_fwd, seg_bwd, w_query, w_key, gain, gossip_exp):
    query_weight = w_query[0, 0]
    key_weight = w_key[0, 0]
    gain_own = gain[0, 0].reshape(1, -1)
    grad_rows = bwd_grad[0, 0]
    count, local = grad_rows.shape
    width = 2 * local
    pipe_count = lax.axis_size("pipe")
    rep_count = lax.axis_size("rep")
    levels = rep_count.bit_length() - 1
    at = lax.axis_index("tp").astype(jnp.int32).reshape(1)
    exponent = gossip_exp[0]

    bwd_other = shifted(bwd_in[0, 0], "tp", 1)
    gain_other = shifted(gain_own, "tp", 1)
    gain_other, fwd_rows = lax.optimization_barrier((gain_other, fwd_in[0, 0]))
    fwd_other = shifted(fwd_rows, "tp", 1)

    q, k, normed, xhat, inv = project(
        at, (bwd_in[0, 0], bwd_other, fwd_in[0, 0], fwd_other), gain_own, gain_other, query_weight, key_weight
    )
    section_out = forward(at, q, k, normed, fwd_in[0, 0], seg_fwd[0, 0])
    q, section_out = lax.optimization_barrier((q, section_out))
    first_rows = shifted(section_out[: count // 2], "pipe", 1)
    dq, dv, key_part = backward(at, q, k, normed, grad_rows, seg_bwd[0, 0])
    dq, first_rows, section_out = lax.optimization_barrier((dq, first_rows, section_out))
    last_rows = shifted(section_out[count // 2 :], "pipe", 1)
    key_other = shifted(key_part.astype(BF16), "tp", 1)
    inward = shifted(away(at, dq, query_weight), "tp", 1)
    dk = (key_part + key_other.astype(F32)).astype(BF16)
    part, gram = home(at, dq, query_weight, dv, dk, key_weight, normed)
    weighted, sums, grad_gain, squares = gather(part, inward, xhat, gain_own, gram)
    last_rows, squares = lax.optimization_barrier((last_rows, squares))
    squares = total_over(squares, "tp")

    bit = jnp.left_shift(gossip_exp, lax.axis_index("pipe").astype(jnp.int32)).astype(F32)
    totals = total_over(jnp.concatenate([squares, bit.reshape(1, 1)], axis=1), "pipe")
    total = pipe_count * (width * width + width * HEAD + width)
    inverse = lax.rsqrt(totals[:, 0:1] / total + STEP_EPS)
    plans = [straight(k, rep_count, pipe_count) for k in range(levels)]
    if rep_count == 4 and pipe_count == 4:
        plans += [crossed(bit, far, rep_count, pipe_count) for bit in range(2) for far in range(2)]
        table = [choices([n >> p & 1 for p in range(pipe_count)]) for n in range(1 << pipe_count)]
        own = jnp.asarray(table, jnp.int32)
        place = totals[0, 1].astype(jnp.int32) * pipe_count + lax.axis_index("pipe")
        exponent = jnp.sum(jnp.where(jnp.arange(own.size) == place, own.reshape(-1), 0))

    back_rows = turn(weighted, xhat, inv, sums, shifted(sums, "tp", 1), grad_rows)
    back_rows, inverse = lax.optimization_barrier((back_rows, inverse))
    prev_rows = shifted(back_rows, "pipe", -1)
    early = step(normed, dq, query_weight, inverse, 0, 2 * width // PIECES)
    values = (at, early, normed, dq, query_weight, dk, key_weight, gain_own, grad_gain, inverse)
    values += (first_rows, last_rows)
    query_out, key_out, gain_out, next_rows = lax.switch(exponent, [partial(swap, plan=plan) for plan in plans], values)
    outs = (next_rows, prev_rows, query_out, key_out, gain_out)
    return tuple(out[None, None] for out in outs)


def solution(mesh):
    rows = P("rep", "pipe", None, "tp")
    tokens = P("rep", "pipe", None)
    keyed = P("rep", "pipe", None, None)
    line = P("rep", "pipe", "tp")
    return jax.shard_map(
        shards,
        mesh=mesh,
        in_specs=(rows, rows, rows, tokens, tokens, rows, keyed, line, P("pipe")),
        out_specs=(rows, rows, rows, keyed, line),
        check_vma=False,
    )
```

```python
from functools import partial

import jax
import jax.numpy as jnp
from jax import lax
from jax.experimental import pallas as pl
from jax.experimental.pallas import tpu as pltpu
from jax.sharding import PartitionSpec as P

HEAD = 128
LN_EPS = 1e-05
STEP_EPS = 1e-06
LEARN_RATE = 0.2
MASK_FILL = -1e30
CHUNK = 16
PIECES = 12
F32 = jnp.float32
BF16 = jnp.bfloat16
LAST = (((1,), (1,)), ((), ()))
FIRST = (((0,), (0,)), ((), ()))
VMEM_LIMIT = 48 * 1024 * 1024


def shifted(block, axis, by):
    length = lax.axis_size(axis)
    return lax.ppermute(block, axis, [(i, (i + by) % length) for i in range(length)])


def total_over(value, axis):
    parts = [shifted(value, axis, by) for by in range(1, lax.axis_size(axis))]
    for part in parts:
        value = value + part
    return value


def dot(a, b, dims=(((1,), (0,)), ((), ()))):
    return lax.dot_general(a, b, dims, preferred_element_type=F32)


def call(kernel, name, grid, prefetch, in_specs, out_specs, out_shape, scratch=(), cost=None):
    return pl.pallas_call(
        kernel,
        name=name,
        grid_spec=pltpu.PrefetchScalarGridSpec(
            num_scalar_prefetch=prefetch,
            grid=grid,
            in_specs=in_specs,
            out_specs=out_specs,
            scratch_shapes=list(scratch),
        ),
        out_shape=out_shape,
        cost_estimate=cost,
        compiler_params=pltpu.CompilerParams(vmem_limit_bytes=VMEM_LIMIT),
    )


def whole(shape):
    return pl.BlockSpec(shape, lambda *_: (0,) * len(shape))


def project_kernel(at, *refs):
    *arrays, gain_own, gain_other, q, k, h, xhat, inv, rows, key_rows, blocks, arrived = refs
    *batches, weight, key_weight = arrays
    count, local = xhat.shape
    width = 2 * local
    scale = width ** (-0.5)
    block = blocks.shape[2]

    def block_copy(j):
        columns = pl.ds(pl.multiple_of(j * block, block), block)
        return pltpu.make_async_copy(weight.at[:, columns], blocks.at[j], arrived.at[len(batches) + 1 + j])

    copies = [pltpu.make_async_copy(ref, rows.at[i], arrived.at[i]) for i, ref in enumerate(batches)]
    copies.append(pltpu.make_async_copy(key_weight, key_rows, arrived.at[len(batches)]))
    for copy in copies:
        copy.start()
    for j in range(blocks.shape[0]):
        block_copy(j).start()

    mine = pl.multiple_of(at[0] * local, HEAD)
    rest = pl.multiple_of((1 - at[0]) * local, HEAD)
    gain_a, gain_b = gain_own[...].astype(F32), gain_other[...].astype(F32)
    for batch in range(2):
        copies[2 * batch].wait()
        copies[2 * batch + 1].wait()

        def some(n, carry):
            part = pl.ds(pl.multiple_of(n * CHUNK, CHUNK), CHUNK)
            a, b = rows[2 * batch, part, :].astype(F32), rows[2 * batch + 1, part, :].astype(F32)
            mean = (jnp.sum(a, axis=1, keepdims=True) + jnp.sum(b, axis=1, keepdims=True)) / width
            a, b = a - mean, b - mean
            var = (jnp.sum(a * a, axis=1, keepdims=True) + jnp.sum(b * b, axis=1, keepdims=True)) / width
            inv_std = lax.rsqrt(var + LN_EPS)
            a, b = a * inv_std, b * inv_std
            to = pl.ds(pl.multiple_of(batch * count + n * CHUNK, CHUNK), CHUNK)
            h[to, pl.ds(mine, local)] = (a * gain_a).astype(BF16)
            h[to, pl.ds(rest, local)] = (b * gain_b).astype(BF16)
            if batch == 0:
                xhat[part, :] = a
                inv[part, :] = inv_std
            return carry

        lax.fori_loop(0, count // CHUNK, some, 0, unroll=4)

    copies[-1].wait()
    k[...] = (dot(h[...], key_rows[...]) * scale).astype(BF16)

    def one(j, carry):
        block_copy(j).wait()
        q[:, pl.ds(pl.multiple_of(j * block, block), block)] = (dot(h[...], blocks[j]) * scale).astype(BF16)
        return carry

    lax.fori_loop(0, blocks.shape[0], one, 0)


def project(at, batches, gain_own, gain_other, weight, key_weight):
    count, local = batches[0].shape
    width = 2 * local
    block = 256
    parts = weight.shape[1] // block
    shapes = [
        jax.ShapeDtypeStruct((2 * count, weight.shape[1]), BF16),
        jax.ShapeDtypeStruct((2 * count, HEAD), BF16),
        jax.ShapeDtypeStruct((2 * count, width), BF16),
        jax.ShapeDtypeStruct((count, local), F32),
        jax.ShapeDtypeStruct((count, 1), F32),
    ]
    return call(
        project_kernel,
        "project",
        (1,),
        1,
        [pl.BlockSpec(memory_space=pl.ANY)] * 6 + [whole((1, local))] * 2,
        [whole(s.shape) for s in shapes],
        shapes,
        scratch=[
            pltpu.VMEM((4, count, local), BF16),
            pltpu.VMEM((width, HEAD), BF16),
            pltpu.VMEM((parts, width, block), BF16),
            pltpu.SemaphoreType.DMA((5 + parts,)),
        ],
        cost=pl.CostEstimate(
            flops=4 * count * width * local, bytes_accessed=2 * weight.size + 16 * count * local, transcendentals=0
        ),
    )(at, *batches, weight, key_weight, gain_own, gain_other)


def softmax(q, k, seg_col, seg_row):
    scores = dot(q, k, LAST) * HEAD ** (-0.5)
    scores = jnp.where(seg_col == seg_row, scores, MASK_FILL)
    expo = jnp.exp(scores - jnp.max(scores, axis=1, keepdims=True))
    return (expo / jnp.sum(expo, axis=1, keepdims=True)).astype(BF16)


def backward_kernel(at, q, k, v, g, seg_col, seg_row, dq, dv, dk):
    @pl.when(pl.program_id(0) == 0)
    def _():
        dk[...] = jnp.zeros_like(dk)

    keys = k[...]
    added = jnp.zeros(dk.shape, F32)
    for start in range(0, q.shape[1], HEAD):
        cols = slice(start, start + HEAD)
        probs = softmax(q[:, cols], keys, seg_col[...], seg_row[...])
        grads = g[:, cols]
        prob_grad = dot(grads, v[:, cols], LAST)
        prob_f = probs.astype(F32)
        inner = jnp.sum(prob_grad * prob_f, axis=1, keepdims=True)
        score_grad = (prob_f * (prob_grad - inner) * HEAD ** (-0.5)).astype(BF16)
        dv[:, cols] = dot(probs, grads, FIRST)
        dq[:, cols] = dot(score_grad, keys).astype(BF16)
        added = added + dot(score_grad, q[:, cols], FIRST)
    dk[...] += added


def heads_at(rows, start, block):
    if start:
        return pl.BlockSpec((rows, block), lambda j, at: (0, j + at[0] * start))
    return pl.BlockSpec((rows, block), lambda j, at: (0, j))


def attention_cost(count, local, products):
    heads = local // HEAD
    return pl.CostEstimate(
        flops=2 * products * heads * count * count * HEAD,
        bytes_accessed=10 * count * local,
        transcendentals=heads * count * count,
    )


def backward(at, q, k, normed, grads, seg, group=6):
    count, local = grads.shape
    block = group * HEAD
    half = local // block
    return call(
        backward_kernel,
        "backward",
        (half,),
        1,
        [
            heads_at(count, 0, block),
            whole((count, HEAD)),
            heads_at(count, half, block),
            heads_at(count, 0, block),
            whole((count, 1)),
            whole((1, count)),
        ],
        [heads_at(count, 0, block), heads_at(count, 0, block), whole((count, HEAD))],
        [
            jax.ShapeDtypeStruct((count, local), BF16),
            jax.ShapeDtypeStruct((count, local), F32),
            jax.ShapeDtypeStruct((count, HEAD), F32),
        ],
        cost=attention_cost(count, local, 5),
    )(at, q, k, normed, grads, seg.reshape(-1, 1), seg.reshape(1, -1))


def forward_kernel(at, q, k, v, x, seg_col, seg_row, upper, lower):
    keys = k[...]
    half = upper.shape[0]
    for start in range(0, q.shape[1], HEAD):
        cols = slice(start, start + HEAD)
        probs = softmax(q[:, cols], keys, seg_col[...], seg_row[...])
        rows = (x[:, cols].astype(F32) + dot(probs, v[:, cols])).astype(BF16)
        upper[:, cols] = rows[:half]
        lower[:, cols] = rows[half:]


def forward(at, q, k, normed, rows, seg, group=6):
    count, local = rows.shape
    block = group * HEAD
    half = local // block
    return call(
        forward_kernel,
        "forward",
        (half,),
        1,
        [
            pl.BlockSpec((count, block), lambda j, at: (1, j)),
            pl.BlockSpec((count, HEAD), lambda j, at: (1, 0)),
            pl.BlockSpec((count, block), lambda j, at: (1, j + at[0] * half)),
            heads_at(count, 0, block),
            whole((count, 1)),
            whole((1, count)),
        ],
        [heads_at(count // 2, 0, block)] * 2,
        [jax.ShapeDtypeStruct((count // 2, local), BF16)] * 2,
        cost=attention_cost(count, local, 2),
    )(at, q, k, normed, rows, seg.reshape(-1, 1), seg.reshape(1, -1))


def away_kernel(at, dq, weight, out):
    out[...] = (dot(dq[...], weight[...], LAST) * (2 * dq.shape[1]) ** (-0.5)).astype(BF16)


def away(at, dq, weight, block=512):
    count, local = dq.shape
    half = local // block
    return call(
        away_kernel,
        "away",
        (half,),
        1,
        [whole((count, local)), pl.BlockSpec((block, local), lambda j, at: (j + (1 - at[0]) * half, 0))],
        pl.BlockSpec((count, block), lambda j, at: (0, j)),
        jax.ShapeDtypeStruct((count, local), BF16),
        cost=pl.CostEstimate(flops=2 * count * local * local, bytes_accessed=2 * local * local, transcendentals=0),
    )(at, dq, weight)


def home_kernel(at, dq, weight, dv, dk, key_weight, normed, out, gram):
    local = dq.shape[1]
    scale = (2 * local) ** (-0.5)
    out[...] = (dot(dq[...], weight[...], LAST) + dot(dk[...], key_weight[...], LAST)) * scale + dv[...]

    @pl.when(pl.program_id(0) == pl.num_programs(0) - 1)
    def _():
        rows = dot(normed[...], normed[...], LAST)
        steps = dot(dq[...], dq[...], LAST) + 0.5 * dot(dk[...], dk[...], LAST)
        part = jnp.sum(rows * steps, axis=0, keepdims=True)
        gram[...] = jnp.sum(part, axis=1, keepdims=True) / (2 * local)


def home(at, dq, weight, dv, dk, key_weight, normed, block=512):
    count, local = dq.shape
    half = local // block
    return call(
        home_kernel,
        "home",
        (half,),
        1,
        [
            whole((count, local)),
            pl.BlockSpec((block, local), lambda j, at: (j + at[0] * half, 0)),
            pl.BlockSpec((count, block), lambda j, at: (0, j)),
            whole((count, HEAD)),
            pl.BlockSpec((block, HEAD), lambda j, at: (j + at[0] * half, 0)),
            pl.BlockSpec((count, 2 * local), lambda j, at: (0, 0)),
        ],
        [pl.BlockSpec((count, block), lambda j, at: (0, j)), whole((1, 1))],
        [jax.ShapeDtypeStruct((count, local), F32), jax.ShapeDtypeStruct((1, 1), F32)],
        cost=pl.CostEstimate(flops=2 * count * local * local, bytes_accessed=2 * local * local, transcendentals=0),
    )(at, dq, weight, dv, dk, key_weight, normed)


def gather_kernel(part, theirs, xhat, gain, gram, weighted, sums, grad_gain, squares):
    @pl.when(pl.program_id(0) == 0)
    def _():
        sums[...] = jnp.zeros_like(sums)
        squares[...] = gram[...]

    grad = part[...] + theirs[...].astype(F32)
    scaled = xhat[...]
    along = jnp.sum(grad * scaled, axis=0, keepdims=True)
    grad_gain[...] = along
    squares[...] += jnp.sum(along * along, axis=1, keepdims=True)
    grad = grad * gain[...].astype(F32)
    weighted[...] = grad
    sums[:, 0:1] += jnp.sum(grad, axis=1, keepdims=True)
    sums[:, 1:2] += jnp.sum(grad * scaled, axis=1, keepdims=True)


def gather(part, theirs, xhat, gain, gram, block=512):
    count, local = part.shape
    wide = pl.BlockSpec((count, block), lambda j: (0, j))
    line = pl.BlockSpec((1, block), lambda j: (0, j))
    return call(
        gather_kernel,
        "gather",
        (local // block,),
        0,
        [wide, wide, wide, line, whole((1, 1))],
        [wide, whole((count, 2)), line, whole((1, 1))],
        [
            jax.ShapeDtypeStruct((count, local), F32),
            jax.ShapeDtypeStruct((count, 2), F32),
            jax.ShapeDtypeStruct((1, local), F32),
            jax.ShapeDtypeStruct((1, 1), F32),
        ],
        cost=pl.CostEstimate(flops=10 * count * local, bytes_accessed=18 * count * local, transcendentals=0),
    )(part, theirs, xhat, gain, gram)


def turn_kernel(weighted, xhat, inv, sums, others, grads, out):
    means = (sums[...] + others[...]) / (2 * xhat.shape[1])
    change = inv[...] * (weighted[...] - means[:, 0:1] - xhat[...] * means[:, 1:2])
    out[...] = (grads[...].astype(F32) + change).astype(BF16)


def turn(weighted, xhat, inv, sums, others, grads):
    count, local = grads.shape
    return call(
        turn_kernel,
        "turn",
        (1,),
        0,
        [whole((count, local)), whole((count, local)), whole((count, 1)), whole((count, 2)), whole((count, 2)), whole((count, local))],
        whole((count, local)),
        jax.ShapeDtypeStruct((count, local), BF16),
        cost=pl.CostEstimate(flops=6 * count * local, bytes_accessed=12 * count * local, transcendentals=0),
    )(weighted, xhat, inv, sums, others, grads)


def step_kernel(scale, normed, grads, weight, inverse, out):
    grad = dot(normed[...], grads[...], FIRST) * scale
    step = (LEARN_RATE * grad * inverse[...]).astype(BF16)
    out[...] = (weight[...].astype(F32) - step.astype(F32)).astype(BF16)


def step(normed, grads, weight, inverse, start, size):
    count, cols = grads.shape
    scale = weight.shape[0] ** (-0.5)
    block = min(size, 256)
    first = start // block
    return call(
        partial(step_kernel, scale),
        "step",
        (size // block,),
        0,
        [
            pl.BlockSpec((count, block), lambda j: (0, j + first)),
            whole((count, cols)),
            pl.BlockSpec((block, cols), lambda j: (j + first, 0)),
            whole((1, 1)),
        ],
        pl.BlockSpec((block, cols), lambda j: (j, 0)),
        jax.ShapeDtypeStruct((size, cols), BF16),
        cost=pl.CostEstimate(flops=2 * size * count * cols, bytes_accessed=4 * size * cols, transcendentals=0),
    )(normed, grads, weight, inverse)


def updated(weight, grad, inverse):
    change = (LEARN_RATE * grad * inverse).astype(BF16)
    return (weight.astype(F32) - change.astype(F32)).astype(BF16)


def small_kernel(at, normed, dk, key_weight, gain, grad_gain, inverse, out):
    local = normed.shape[1]
    grad = dot(normed[...], dk[...], FIRST) * (2 * local) ** (-0.5)
    out[:local, :] = updated(key_weight[...], grad, inverse[...])
    line = updated(gain[...], grad_gain[...], inverse[...]).astype(F32)
    rows = [line[:, s : s + HEAD] for s in range(0, local, HEAD)]
    rows.append(jnp.zeros((-len(rows) % 16, HEAD), F32))
    out[local:, :] = jnp.concatenate(rows, axis=0).astype(BF16)


def small_step(at, normed, dk, key_weight, gain, grad_gain, inverse):
    count = dk.shape[0]
    local = gain.shape[1]
    rows = local + -(-local // HEAD // 16) * 16
    return call(
        small_kernel,
        "small_step",
        (1,),
        1,
        [
            pl.BlockSpec((count, local), lambda j, at: (0, at[0])),
            whole((count, HEAD)),
            pl.BlockSpec((local, HEAD), lambda j, at: (at[0], 0)),
            whole((1, local)),
            whole((1, local)),
            whole((1, 1)),
        ],
        whole((rows, HEAD)),
        jax.ShapeDtypeStruct((rows, HEAD), BF16),
        cost=pl.CostEstimate(flops=2 * count * local * HEAD, bytes_accessed=2 * count * local, transcendentals=0),
    )(at, normed, dk, key_weight, gain, grad_gain, inverse)


def halves(mine, theirs):
    return ((mine.astype(F32) + theirs.astype(F32)) * 0.5).astype(BF16)


def halves_kernel(mine, theirs, *rest):
    rest[-1][...] = halves(mine[...], theirs[...])


def halves_into(whole_out, mine, theirs, start, rows):
    size, cols = mine.shape
    block = min(size, 128)
    first = start // block
    part = pl.BlockSpec((block, cols), lambda j: (j, 0))
    earlier = [] if whole_out is None else [whole_out]
    return pl.pallas_call(
        halves_kernel,
        name="halves",
        grid=(size // block,),
        in_specs=[part, part] + [pl.BlockSpec(memory_space=pl.ANY)] * len(earlier),
        out_specs=pl.BlockSpec((block, cols), lambda j: (j + first, 0)),
        out_shape=jax.ShapeDtypeStruct((rows, cols), BF16),
        input_output_aliases={2: 0} if earlier else {},
        cost_estimate=pl.CostEstimate(flops=2 * size * cols, bytes_accessed=6 * size * cols, transcendentals=0),
    )(mine, theirs, *earlier)


def column(p, level, rep_count, pipe_count):
    return [
        (r * pipe_count + p, (r ^ 1 << level) * pipe_count + p) for r in range(rep_count) if r ^ 1 << level < rep_count
    ]


def traded(mask, pipe_count):
    return [
        (r * pipe_count + p, r * pipe_count + (p ^ mask if r in (1, 2) else p)) for r in range(4) for p in range(pipe_count)
    ]


def sent(exponents, mask, pipe_count):
    hops = []
    for p, k in enumerate(exponents):
        q = p ^ mask
        hops += [(r * pipe_count + p, (r ^ 1 << k) * pipe_count + p) for r in (0, 3)]
        hops += [(r * pipe_count + p, (r ^ 1 << exponents[q]) * pipe_count + q) for r in (1, 2)]
    return hops


def straight(level, rep_count, pipe_count):
    send = [hop for p in range(pipe_count) for hop in column(p, level, rep_count, pipe_count)]
    return send, None, send


def crossed(bit, far_bit, rep_count, pipe_count):
    exponents = [int(p >> bit & 1 == far_bit) for p in range(pipe_count)]
    direct = [hop for p, k in enumerate(exponents) for hop in column(p, k, rep_count, pipe_count)]
    return direct, traded(1 << bit, pipe_count), sent(exponents, 1 << bit, pipe_count)


def choices(exponents):
    count = len(exponents)
    best = None
    for axes in range(1 << count):
        taken, pairs = list(exponents), 0
        for p, k in enumerate(exponents):
            bit = axes >> p & 1
            other = p ^ 1 << bit
            if axes >> other & 1 == bit and exponents[other] != k:
                far = p if k == 1 else other
                taken[p] = 2 + 2 * bit + (far >> bit & 1)
                pairs += 1
        if best is None or pairs > best[0]:
            best = (pairs, taken)
    return best[1]


def exchanged(first, chains, plan, token, take):
    axes = ("rep", "pipe")
    direct, trade, send = plan
    moved, landed, last, merged = [None, None], [None, None], [None, None], None
    made = [[], []]
    received = lax.ppermute(first, axes, direct)
    for at in range(max(len(blocks) for blocks in chains) + 1):
        for c, blocks in enumerate(chains):
            if at > len(blocks):
                continue
            going = None
            if at < len(blocks):
                made[c].append(blocks[at](token))
                going = made[c][-1]
            tied = merged if at > 3 else None
            parts = [going, moved[c], landed[c], last[1 - c], tied]
            parts += [token if (at, c) == (1, 1) else None, received if (at, c) == (1, 0) else None]
            held = iter(lax.optimization_barrier([part for part in parts if part is not None]))
            parts = [None if part is None else next(held) for part in parts]
            going, moved[c], landed[c], ready = parts[:4]
            merged, token, received = [a if b is None else b for a, b in zip((merged, token, received), parts[4:])]
            if (at, c) == (1, 0):
                merged = take(merged, None, None, first, received)
            if ready is not None:
                number = at - 3 + c
                merged = take(merged, 1 - c, number, made[1 - c][number], ready)
            if last[c] is not None:
                merged = take(merged, c, at - 3, made[c][at - 3], last[c])
            last[1 - c], last[c] = None, landed[c]
            landed[c] = None if moved[c] is None else lax.ppermute(moved[c], axes, send)
            if going is not None and trade is not None:
                going = lax.ppermute(going, axes, trade)
            moved[c] = going
    for c, blocks in enumerate(chains):
        if last[c] is not None:
            merged = take(merged, c, len(blocks) - 2, made[c][-2], last[c])
        merged = take(merged, c, len(blocks) - 1, made[c][-1], landed[c])
    return merged


def swap(values, plan):
    at, early, normed, dq, query_weight, dk, key_weight, gain_own, grad_gain, inverse, *next_rows = values
    count, local = dq.shape
    width = 2 * local
    piece = early.shape[0] // 2
    split = 4 * piece
    made = {}

    def stepped(start, size):
        def make(token):
            low, high = (0, 2 * piece) if start < 2 * piece else (2 * piece, split) if start < split else (split, width)
            if low not in made:
                made[low] = step(normed, dq, query_weight, token, low, high - low) if low else early
            return lax.slice_in_dim(made[low], start - low, start - low + size, axis=0)

        return make

    short = piece // 2
    if plan[1] is None:
        head = piece
        evens = [(piece, piece)] + [(s, 2 * piece) for s in range(split, width, 4 * piece)]
        odds = [(s, 2 * piece) for s in range(2 * piece, width, 4 * piece)]
        odds.insert(-1, None)
    else:
        head = short
        end = width - piece
        evens = [(short, short)] + [(s, piece) for s in range(2 * piece, end, 2 * piece)] + [(end + short, short)]
        odds = [(s, piece) for s in range(piece, end, 2 * piece)] + [None, (end, short)]
    chains = [
        [
            stepped(*spot)
            if spot
            else lambda token: small_step(at, normed, dk, key_weight, gain_own, grad_gain, token)
            for spot in spots
        ]
        for spots in (evens, odds)
    ]
    small_out = []

    def take(merged, c, n, block, received):
        spot = (0, head) if c is None else (evens, odds)[c][n]
        if spot is None:
            small_out.append(halves(block, received))
            return merged
        return halves_into(merged, block, received, spot[0], width)

    merged = exchanged(lax.slice_in_dim(early, 0, head, axis=0), chains, plan, inverse, take)
    small_out = small_out[0]
    mine = small_out[:local]
    theirs = shifted(mine, "tp", 1)
    key_out = jnp.where(
        at[0] == 0, jnp.concatenate([mine, theirs], axis=0), jnp.concatenate([theirs, mine], axis=0)
    )
    gain_out = small_out[local : local + local // HEAD].reshape(-1)
    return merged, key_out, gain_out, jnp.concatenate(next_rows, axis=0)


def shards(fwd_in, bwd_in, bwd_grad, seg_fwd, seg_bwd, w_query, w_key, gain, gossip_exp):
    query_weight = w_query[0, 0]
    key_weight = w_key[0, 0]
    gain_own = gain[0, 0].reshape(1, -1)
    grad_rows = bwd_grad[0, 0]
    count, local = grad_rows.shape
    width = 2 * local
    pipe_count = lax.axis_size("pipe")
    rep_count = lax.axis_size("rep")
    levels = rep_count.bit_length() - 1
    at = lax.axis_index("tp").astype(jnp.int32).reshape(1)
    exponent = gossip_exp[0]

    bwd_other = shifted(bwd_in[0, 0], "tp", 1)
    gain_other = shifted(gain_own, "tp", 1)
    gain_other, fwd_rows = lax.optimization_barrier((gain_other, fwd_in[0, 0]))
    fwd_other = shifted(fwd_rows, "tp", 1)

    q, k, normed, xhat, inv = project(
        at, (bwd_in[0, 0], bwd_other, fwd_in[0, 0], fwd_other), gain_own, gain_other, query_weight, key_weight
    )
    first_rows, last_rows = forward(at, q, k, normed, fwd_in[0, 0], seg_fwd[0, 0])
    q, first_rows, last_rows = lax.optimization_barrier((q, first_rows, last_rows))
    first_rows = shifted(first_rows, "pipe", 1)
    dq, dv, key_part = backward(at, q, k, normed, grad_rows, seg_bwd[0, 0])
    dq, first_rows, last_rows = lax.optimization_barrier((dq, first_rows, last_rows))
    last_rows = shifted(last_rows, "pipe", 1)
    key_other = shifted(key_part.astype(BF16), "tp", 1)
    inward = shifted(away(at, dq, query_weight), "tp", 1)
    dk = (key_part + key_other.astype(F32)).astype(BF16)
    part, gram = home(at, dq, query_weight, dv, dk, key_weight, normed)
    weighted, sums, grad_gain, squares = gather(part, inward, xhat, gain_own, gram)
    last_rows, squares = lax.optimization_barrier((last_rows, squares))
    squares = total_over(squares, "tp")

    bit = jnp.left_shift(gossip_exp, lax.axis_index("pipe").astype(jnp.int32)).astype(F32)
    totals = total_over(jnp.concatenate([squares, bit.reshape(1, 1)], axis=1), "pipe")
    total = pipe_count * (width * width + width * HEAD + width)
    inverse = lax.rsqrt(totals[:, 0:1] / total + STEP_EPS)
    plans = [straight(k, rep_count, pipe_count) for k in range(levels)]
    if rep_count == 4 and pipe_count == 4:
        plans += [crossed(bit, far, rep_count, pipe_count) for bit in range(2) for far in range(2)]
        table = [choices([n >> p & 1 for p in range(pipe_count)]) for n in range(1 << pipe_count)]
        own = jnp.asarray(table, jnp.int32)
        place = totals[0, 1].astype(jnp.int32) * pipe_count + lax.axis_index("pipe")
        exponent = jnp.sum(jnp.where(jnp.arange(own.size) == place, own.reshape(-1), 0))

    back_rows = turn(weighted, xhat, inv, sums, shifted(sums, "tp", 1), grad_rows)
    back_rows, inverse = lax.optimization_barrier((back_rows, inverse))
    prev_rows = shifted(back_rows, "pipe", -1)
    early = step(normed, dq, query_weight, inverse, 0, 2 * width // PIECES)
    values = (at, early, normed, dq, query_weight, dk, key_weight, gain_own, grad_gain, inverse)
    values += (first_rows, last_rows)
    query_out, key_out, gain_out, next_rows = lax.switch(exponent, [partial(swap, plan=plan) for plan in plans], values)
    outs = (next_rows, prev_rows, query_out, key_out, gain_out)
    return tuple(out[None, None] for out in outs)


def solution(mesh):
    rows = P("rep", "pipe", None, "tp")
    tokens = P("rep", "pipe", None)
    keyed = P("rep", "pipe", None, None)
    line = P("rep", "pipe", "tp")
    return jax.shard_map(
        shards,
        mesh=mesh,
        in_specs=(rows, rows, rows, tokens, tokens, rows, keyed, line, P("pipe")),
        out_specs=(rows, rows, rows, keyed, line),
        check_vma=False,
    )
```

```python
from functools import partial

import jax
import jax.numpy as jnp
from jax import lax
from jax.experimental import pallas as pl
from jax.experimental.pallas import tpu as pltpu
from jax.sharding import PartitionSpec as P

HEAD = 128
LN_EPS = 1e-05
STEP_EPS = 1e-06
LEARN_RATE = 0.2
MASK_FILL = -1e30
CHUNK = 16
PIECES = 12
F32 = jnp.float32
BF16 = jnp.bfloat16
LAST = (((1,), (1,)), ((), ()))
FIRST = (((0,), (0,)), ((), ()))
VMEM_LIMIT = 48 * 1024 * 1024


def shifted(block, axis, by):
    length = lax.axis_size(axis)
    return lax.ppermute(block, axis, [(i, (i + by) % length) for i in range(length)])


def total_over(value, axis):
    parts = [shifted(value, axis, by) for by in range(1, lax.axis_size(axis))]
    for part in parts:
        value = value + part
    return value


def dot(a, b, dims=(((1,), (0,)), ((), ()))):
    return lax.dot_general(a, b, dims, preferred_element_type=F32)


def call(kernel, name, grid, prefetch, in_specs, out_specs, out_shape, scratch=(), cost=None):
    return pl.pallas_call(
        kernel,
        name=name,
        grid_spec=pltpu.PrefetchScalarGridSpec(
            num_scalar_prefetch=prefetch,
            grid=grid,
            in_specs=in_specs,
            out_specs=out_specs,
            scratch_shapes=list(scratch),
        ),
        out_shape=out_shape,
        cost_estimate=cost,
        compiler_params=pltpu.CompilerParams(vmem_limit_bytes=VMEM_LIMIT),
    )


def whole(shape):
    return pl.BlockSpec(shape, lambda *_: (0,) * len(shape))


def project_kernel(at, *refs):
    *arrays, gain_own, gain_other, q, k, h, xhat, inv, rows, key_rows, blocks, arrived = refs
    *batches, weight, key_weight = arrays
    count, local = xhat.shape
    width = 2 * local
    scale = width ** (-0.5)
    block = blocks.shape[2]

    def block_copy(j):
        columns = pl.ds(pl.multiple_of(j * block, block), block)
        return pltpu.make_async_copy(weight.at[:, columns], blocks.at[j], arrived.at[len(batches) + 1 + j])

    copies = [pltpu.make_async_copy(ref, rows.at[i], arrived.at[i]) for i, ref in enumerate(batches)]
    copies.append(pltpu.make_async_copy(key_weight, key_rows, arrived.at[len(batches)]))
    for copy in copies:
        copy.start()
    for j in range(blocks.shape[0]):
        block_copy(j).start()

    mine = pl.multiple_of(at[0] * local, HEAD)
    rest = pl.multiple_of((1 - at[0]) * local, HEAD)
    gain_a, gain_b = gain_own[...].astype(F32), gain_other[...].astype(F32)
    for batch in range(2):
        copies[2 * batch].wait()
        copies[2 * batch + 1].wait()

        def some(n, carry):
            part = pl.ds(pl.multiple_of(n * CHUNK, CHUNK), CHUNK)
            a, b = rows[2 * batch, part, :].astype(F32), rows[2 * batch + 1, part, :].astype(F32)
            mean = (jnp.sum(a, axis=1, keepdims=True) + jnp.sum(b, axis=1, keepdims=True)) / width
            a, b = a - mean, b - mean
            var = (jnp.sum(a * a, axis=1, keepdims=True) + jnp.sum(b * b, axis=1, keepdims=True)) / width
            inv_std = lax.rsqrt(var + LN_EPS)
            a, b = a * inv_std, b * inv_std
            to = pl.ds(pl.multiple_of(batch * count + n * CHUNK, CHUNK), CHUNK)
            h[to, pl.ds(mine, local)] = (a * gain_a).astype(BF16)
            h[to, pl.ds(rest, local)] = (b * gain_b).astype(BF16)
            if batch == 0:
                xhat[part, :] = a
                inv[part, :] = inv_std
            return carry

        lax.fori_loop(0, count // CHUNK, some, 0, unroll=4)

    copies[-1].wait()
    k[...] = (dot(h[...], key_rows[...]) * scale).astype(BF16)

    def one(j, carry):
        block_copy(j).wait()
        q[:, pl.ds(pl.multiple_of(j * block, block), block)] = (dot(h[...], blocks[j]) * scale).astype(BF16)
        return carry

    lax.fori_loop(0, blocks.shape[0], one, 0)


def project(at, batches, gain_own, gain_other, weight, key_weight):
    count, local = batches[0].shape
    width = 2 * local
    block = 256
    parts = weight.shape[1] // block
    shapes = [
        jax.ShapeDtypeStruct((2 * count, weight.shape[1]), BF16),
        jax.ShapeDtypeStruct((2 * count, HEAD), BF16),
        jax.ShapeDtypeStruct((2 * count, width), BF16),
        jax.ShapeDtypeStruct((count, local), F32),
        jax.ShapeDtypeStruct((count, 1), F32),
    ]
    return call(
        project_kernel,
        "project",
        (1,),
        1,
        [pl.BlockSpec(memory_space=pl.ANY)] * 6 + [whole((1, local))] * 2,
        [whole(s.shape) for s in shapes],
        shapes,
        scratch=[
            pltpu.VMEM((4, count, local), BF16),
            pltpu.VMEM((width, HEAD), BF16),
            pltpu.VMEM((parts, width, block), BF16),
            pltpu.SemaphoreType.DMA((5 + parts,)),
        ],
        cost=pl.CostEstimate(
            flops=4 * count * width * local, bytes_accessed=2 * weight.size + 16 * count * local, transcendentals=0
        ),
    )(at, *batches, weight, key_weight, gain_own, gain_other)


def softmax(q, k, seg_col, seg_row):
    scores = dot(q, k, LAST) * HEAD ** (-0.5)
    scores = jnp.where(seg_col == seg_row, scores, MASK_FILL)
    expo = jnp.exp(scores - jnp.max(scores, axis=1, keepdims=True))
    return (expo / jnp.sum(expo, axis=1, keepdims=True)).astype(BF16)


def backward_kernel(at, q, k, v, g, seg_col, seg_row, dq, dv, dk):
    @pl.when(pl.program_id(0) == 0)
    def _():
        dk[...] = jnp.zeros_like(dk)

    keys = k[...]
    added = jnp.zeros(dk.shape, F32)
    for start in range(0, q.shape[1], HEAD):
        cols = slice(start, start + HEAD)
        probs = softmax(q[:, cols], keys, seg_col[...], seg_row[...])
        grads = g[:, cols]
        prob_grad = dot(grads, v[:, cols], LAST)
        prob_f = probs.astype(F32)
        inner = jnp.sum(prob_grad * prob_f, axis=1, keepdims=True)
        score_grad = (prob_f * (prob_grad - inner) * HEAD ** (-0.5)).astype(BF16)
        dv[:, cols] = dot(probs, grads, FIRST)
        dq[:, cols] = dot(score_grad, keys).astype(BF16)
        added = added + dot(score_grad, q[:, cols], FIRST)
    dk[...] += added


def heads_at(rows, start, block):
    if start:
        return pl.BlockSpec((rows, block), lambda j, at: (0, j + at[0] * start))
    return pl.BlockSpec((rows, block), lambda j, at: (0, j))


def attention_cost(count, local, products):
    heads = local // HEAD
    return pl.CostEstimate(
        flops=2 * products * heads * count * count * HEAD,
        bytes_accessed=10 * count * local,
        transcendentals=heads * count * count,
    )


def backward(at, q, k, normed, grads, seg, group=6):
    count, local = grads.shape
    block = group * HEAD
    half = local // block
    return call(
        backward_kernel,
        "backward",
        (half,),
        1,
        [
            heads_at(count, 0, block),
            whole((count, HEAD)),
            heads_at(count, half, block),
            heads_at(count, 0, block),
            whole((count, 1)),
            whole((1, count)),
        ],
        [heads_at(count, 0, block), heads_at(count, 0, block), whole((count, HEAD))],
        [
            jax.ShapeDtypeStruct((count, local), BF16),
            jax.ShapeDtypeStruct((count, local), F32),
            jax.ShapeDtypeStruct((count, HEAD), F32),
        ],
        cost=attention_cost(count, local, 5),
    )(at, q, k, normed, grads, seg.reshape(-1, 1), seg.reshape(1, -1))


def forward_kernel(at, q, k, v, x, seg_col, seg_row, upper, lower):
    keys = k[...]
    half = upper.shape[0]
    for start in range(0, q.shape[1], HEAD):
        cols = slice(start, start + HEAD)
        probs = softmax(q[:, cols], keys, seg_col[...], seg_row[...])
        rows = (x[:, cols].astype(F32) + dot(probs, v[:, cols])).astype(BF16)
        upper[:, cols] = rows[:half]
        lower[:, cols] = rows[half:]


def forward(at, q, k, normed, rows, seg, group=6):
    count, local = rows.shape
    block = group * HEAD
    half = local // block
    return call(
        forward_kernel,
        "forward",
        (half,),
        1,
        [
            pl.BlockSpec((count, block), lambda j, at: (1, j)),
            pl.BlockSpec((count, HEAD), lambda j, at: (1, 0)),
            pl.BlockSpec((count, block), lambda j, at: (1, j + at[0] * half)),
            heads_at(count, 0, block),
            whole((count, 1)),
            whole((1, count)),
        ],
        [heads_at(count // 2, 0, block)] * 2,
        [jax.ShapeDtypeStruct((count // 2, local), BF16)] * 2,
        cost=attention_cost(count, local, 2),
    )(at, q, k, normed, rows, seg.reshape(-1, 1), seg.reshape(1, -1))


def away_kernel(at, dq, weight, out):
    out[...] = (dot(dq[...], weight[...], LAST) * (2 * dq.shape[1]) ** (-0.5)).astype(BF16)


def away(at, dq, weight, block=512):
    count, local = dq.shape
    half = local // block
    return call(
        away_kernel,
        "away",
        (half,),
        1,
        [whole((count, local)), pl.BlockSpec((block, local), lambda j, at: (j + (1 - at[0]) * half, 0))],
        pl.BlockSpec((count, block), lambda j, at: (0, j)),
        jax.ShapeDtypeStruct((count, local), BF16),
        cost=pl.CostEstimate(flops=2 * count * local * local, bytes_accessed=2 * local * local, transcendentals=0),
    )(at, dq, weight)


def home_kernel(at, dq, weight, dv, dk, key_weight, normed, out, gram):
    local = dq.shape[1]
    scale = (2 * local) ** (-0.5)
    out[...] = (dot(dq[...], weight[...], LAST) + dot(dk[...], key_weight[...], LAST)) * scale + dv[...]

    @pl.when(pl.program_id(0) == pl.num_programs(0) - 1)
    def _():
        rows = dot(normed[...], normed[...], LAST)
        steps = dot(dq[...], dq[...], LAST) + 0.5 * dot(dk[...], dk[...], LAST)
        part = jnp.sum(rows * steps, axis=0, keepdims=True)
        gram[...] = jnp.sum(part, axis=1, keepdims=True) / (2 * local)


def home(at, dq, weight, dv, dk, key_weight, normed, block=512):
    count, local = dq.shape
    half = local // block
    return call(
        home_kernel,
        "home",
        (half,),
        1,
        [
            whole((count, local)),
            pl.BlockSpec((block, local), lambda j, at: (j + at[0] * half, 0)),
            pl.BlockSpec((count, block), lambda j, at: (0, j)),
            whole((count, HEAD)),
            pl.BlockSpec((block, HEAD), lambda j, at: (j + at[0] * half, 0)),
            pl.BlockSpec((count, 2 * local), lambda j, at: (0, 0)),
        ],
        [pl.BlockSpec((count, block), lambda j, at: (0, j)), whole((1, 1))],
        [jax.ShapeDtypeStruct((count, local), F32), jax.ShapeDtypeStruct((1, 1), F32)],
        cost=pl.CostEstimate(flops=2 * count * local * local, bytes_accessed=2 * local * local, transcendentals=0),
    )(at, dq, weight, dv, dk, key_weight, normed)


def gather_kernel(part, theirs, xhat, gain, gram, weighted, sums, grad_gain, squares):
    @pl.when(pl.program_id(0) == 0)
    def _():
        sums[...] = jnp.zeros_like(sums)
        squares[...] = gram[...]

    grad = part[...] + theirs[...].astype(F32)
    scaled = xhat[...]
    along = jnp.sum(grad * scaled, axis=0, keepdims=True)
    grad_gain[...] = along
    squares[...] += jnp.sum(along * along, axis=1, keepdims=True)
    grad = grad * gain[...].astype(F32)
    weighted[...] = grad
    sums[:, 0:1] += jnp.sum(grad, axis=1, keepdims=True)
    sums[:, 1:2] += jnp.sum(grad * scaled, axis=1, keepdims=True)


def gather(part, theirs, xhat, gain, gram, block=512):
    count, local = part.shape
    wide = pl.BlockSpec((count, block), lambda j: (0, j))
    line = pl.BlockSpec((1, block), lambda j: (0, j))
    return call(
        gather_kernel,
        "gather",
        (local // block,),
        0,
        [wide, wide, wide, line, whole((1, 1))],
        [wide, whole((count, 2)), line, whole((1, 1))],
        [
            jax.ShapeDtypeStruct((count, local), F32),
            jax.ShapeDtypeStruct((count, 2), F32),
            jax.ShapeDtypeStruct((1, local), F32),
            jax.ShapeDtypeStruct((1, 1), F32),
        ],
        cost=pl.CostEstimate(flops=10 * count * local, bytes_accessed=18 * count * local, transcendentals=0),
    )(part, theirs, xhat, gain, gram)


def turn_kernel(weighted, xhat, inv, sums, others, grads, out):
    means = (sums[...] + others[...]) / (2 * xhat.shape[1])
    change = inv[...] * (weighted[...] - means[:, 0:1] - xhat[...] * means[:, 1:2])
    out[...] = (grads[...].astype(F32) + change).astype(BF16)


def turn(weighted, xhat, inv, sums, others, grads):
    count, local = grads.shape
    return call(
        turn_kernel,
        "turn",
        (1,),
        0,
        [whole((count, local)), whole((count, local)), whole((count, 1)), whole((count, 2)), whole((count, 2)), whole((count, local))],
        whole((count, local)),
        jax.ShapeDtypeStruct((count, local), BF16),
        cost=pl.CostEstimate(flops=6 * count * local, bytes_accessed=12 * count * local, transcendentals=0),
    )(weighted, xhat, inv, sums, others, grads)


def step_kernel(scale, normed, grads, weight, inverse, out):
    grad = dot(normed[...], grads[...], FIRST) * scale
    step = (LEARN_RATE * grad * inverse[...]).astype(BF16)
    out[...] = (weight[...].astype(F32) - step.astype(F32)).astype(BF16)


def step(normed, grads, weight, inverse, start, size):
    count, cols = grads.shape
    scale = weight.shape[0] ** (-0.5)
    block = min(size, 256)
    first = start // block
    return call(
        partial(step_kernel, scale),
        "step",
        (size // block,),
        0,
        [
            pl.BlockSpec((count, block), lambda j: (0, j + first)),
            whole((count, cols)),
            pl.BlockSpec((block, cols), lambda j: (j + first, 0)),
            whole((1, 1)),
        ],
        pl.BlockSpec((block, cols), lambda j: (j, 0)),
        jax.ShapeDtypeStruct((size, cols), BF16),
        cost=pl.CostEstimate(flops=2 * size * count * cols, bytes_accessed=4 * size * cols, transcendentals=0),
    )(normed, grads, weight, inverse)


def updated(weight, grad, inverse):
    change = (LEARN_RATE * grad * inverse).astype(BF16)
    return (weight.astype(F32) - change.astype(F32)).astype(BF16)


def small_kernel(at, normed, dk, key_weight, gain, grad_gain, inverse, out):
    local = normed.shape[1]
    grad = dot(normed[...], dk[...], FIRST) * (2 * local) ** (-0.5)
    out[:local, :] = updated(key_weight[...], grad, inverse[...])
    line = updated(gain[...], grad_gain[...], inverse[...]).astype(F32)
    rows = [line[:, s : s + HEAD] for s in range(0, local, HEAD)]
    rows.append(jnp.zeros((-len(rows) % 16, HEAD), F32))
    out[local:, :] = jnp.concatenate(rows, axis=0).astype(BF16)


def small_step(at, normed, dk, key_weight, gain, grad_gain, inverse):
    count = dk.shape[0]
    local = gain.shape[1]
    rows = local + -(-local // HEAD // 16) * 16
    return call(
        small_kernel,
        "small_step",
        (1,),
        1,
        [
            pl.BlockSpec((count, local), lambda j, at: (0, at[0])),
            whole((count, HEAD)),
            pl.BlockSpec((local, HEAD), lambda j, at: (at[0], 0)),
            whole((1, local)),
            whole((1, local)),
            whole((1, 1)),
        ],
        whole((rows, HEAD)),
        jax.ShapeDtypeStruct((rows, HEAD), BF16),
        cost=pl.CostEstimate(flops=2 * count * local * HEAD, bytes_accessed=2 * count * local, transcendentals=0),
    )(at, normed, dk, key_weight, gain, grad_gain, inverse)


def halves(mine, theirs):
    return ((mine.astype(F32) + theirs.astype(F32)) * 0.5).astype(BF16)


def halves_kernel(mine, theirs, *rest):
    rest[-1][...] = halves(mine[...], theirs[...])


def halves_into(whole_out, mine, theirs, start, rows):
    size, cols = mine.shape
    block = min(size, 128)
    first = start // block
    part = pl.BlockSpec((block, cols), lambda j: (j, 0))
    earlier = [] if whole_out is None else [whole_out]
    return pl.pallas_call(
        halves_kernel,
        name="halves",
        grid=(size // block,),
        in_specs=[part, part] + [pl.BlockSpec(memory_space=pl.ANY)] * len(earlier),
        out_specs=pl.BlockSpec((block, cols), lambda j: (j + first, 0)),
        out_shape=jax.ShapeDtypeStruct((rows, cols), BF16),
        input_output_aliases={2: 0} if earlier else {},
        cost_estimate=pl.CostEstimate(flops=2 * size * cols, bytes_accessed=6 * size * cols, transcendentals=0),
    )(mine, theirs, *earlier)


def column(p, level, rep_count, pipe_count):
    return [
        (r * pipe_count + p, (r ^ 1 << level) * pipe_count + p) for r in range(rep_count) if r ^ 1 << level < rep_count
    ]


def traded(mask, pipe_count):
    return [
        (r * pipe_count + p, r * pipe_count + (p ^ mask if r in (1, 2) else p)) for r in range(4) for p in range(pipe_count)
    ]


def sent(exponents, mask, pipe_count):
    hops = []
    for p, k in enumerate(exponents):
        q = p ^ mask
        hops += [(r * pipe_count + p, (r ^ 1 << k) * pipe_count + p) for r in (0, 3)]
        hops += [(r * pipe_count + p, (r ^ 1 << exponents[q]) * pipe_count + q) for r in (1, 2)]
    return hops


def straight(level, rep_count, pipe_count):
    send = [hop for p in range(pipe_count) for hop in column(p, level, rep_count, pipe_count)]
    return send, None, send


def crossed(bit, far_bit, rep_count, pipe_count):
    exponents = [int(p >> bit & 1 == far_bit) for p in range(pipe_count)]
    direct = [hop for p, k in enumerate(exponents) for hop in column(p, k, rep_count, pipe_count)]
    return direct, traded(1 << bit, pipe_count), sent(exponents, 1 << bit, pipe_count)


def choices(exponents):
    count = len(exponents)
    best = None
    for axes in reversed(range(1 << count)):
        taken, pairs = list(exponents), 0
        for p, k in enumerate(exponents):
            bit = axes >> p & 1
            other = p ^ 1 << bit
            if axes >> other & 1 == bit and exponents[other] != k:
                far = p if k == 1 else other
                taken[p] = 2 + 2 * bit + (far >> bit & 1)
                pairs += 1
        if best is None or pairs > best[0]:
            best = (pairs, taken)
    return best[1]


def exchanged(first, chains, plan, token, take):
    axes = ("rep", "pipe")
    direct, trade, send = plan
    moved, landed, last, merged = [None, None], [None, None], [None, None], None
    made = [[], []]
    received = lax.ppermute(first, axes, direct)
    for at in range(max(len(blocks) for blocks in chains) + 1):
        for c, blocks in enumerate(chains):
            if at > len(blocks):
                continue
            going = None
            if at < len(blocks):
                made[c].append(blocks[at](token))
                going = made[c][-1]
            tied = merged if at > 3 else None
            parts = [going, moved[c], landed[c], last[1 - c], tied]
            parts += [token if (at, c) == (1, 1) else None, received if (at, c) == (1, 0) else None]
            held = iter(lax.optimization_barrier([part for part in parts if part is not None]))
            parts = [None if part is None else next(held) for part in parts]
            going, moved[c], landed[c], ready = parts[:4]
            merged, token, received = [a if b is None else b for a, b in zip((merged, token, received), parts[4:])]
            if (at, c) == (1, 0):
                merged = take(merged, None, None, first, received)
            if ready is not None:
                number = at - 3 + c
                merged = take(merged, 1 - c, number, made[1 - c][number], ready)
            if last[c] is not None:
                merged = take(merged, c, at - 3, made[c][at - 3], last[c])
            last[1 - c], last[c] = None, landed[c]
            landed[c] = None if moved[c] is None else lax.ppermute(moved[c], axes, send)
            if going is not None and trade is not None:
                going = lax.ppermute(going, axes, trade)
            moved[c] = going
    for c, blocks in enumerate(chains):
        if last[c] is not None:
            merged = take(merged, c, len(blocks) - 2, made[c][-2], last[c])
        merged = take(merged, c, len(blocks) - 1, made[c][-1], landed[c])
    return merged


def swap(values, plan):
    at, early, normed, dq, query_weight, dk, key_weight, gain_own, grad_gain, inverse, *next_rows = values
    count, local = dq.shape
    width = 2 * local
    piece = early.shape[0] // 2
    split = 4 * piece
    made = {}

    def stepped(start, size):
        def make(token):
            low, high = (0, 2 * piece) if start < 2 * piece else (2 * piece, split) if start < split else (split, width)
            if low not in made:
                made[low] = step(normed, dq, query_weight, token, low, high - low) if low else early
            return lax.slice_in_dim(made[low], start - low, start - low + size, axis=0)

        return make

    short = piece // 2
    if plan[1] is None:
        head = piece
        evens = [(piece, piece)] + [(s, 2 * piece) for s in range(split, width, 4 * piece)]
        odds = [(s, 2 * piece) for s in range(2 * piece, width, 4 * piece)]
        odds.insert(-1, None)
    else:
        head = short
        end = width - piece
        evens = [(short, short)] + [(s, piece) for s in range(2 * piece, end, 2 * piece)] + [(end + short, short)]
        odds = [(s, piece) for s in range(piece, end, 2 * piece)] + [None, (end, short)]
    chains = [
        [
            stepped(*spot)
            if spot
            else lambda token: small_step(at, normed, dk, key_weight, gain_own, grad_gain, token)
            for spot in spots
        ]
        for spots in (evens, odds)
    ]
    small_out = []

    def take(merged, c, n, block, received):
        spot = (0, head) if c is None else (evens, odds)[c][n]
        if spot is None:
            small_out.append(halves(block, received))
            return merged
        return halves_into(merged, block, received, spot[0], width)

    merged = exchanged(lax.slice_in_dim(early, 0, head, axis=0), chains, plan, inverse, take)
    small_out = small_out[0]
    mine = small_out[:local]
    theirs = shifted(mine, "tp", 1)
    key_out = jnp.where(
        at[0] == 0, jnp.concatenate([mine, theirs], axis=0), jnp.concatenate([theirs, mine], axis=0)
    )
    gain_out = small_out[local : local + local // HEAD].reshape(-1)
    return merged, key_out, gain_out, jnp.concatenate(next_rows, axis=0)


def shards(fwd_in, bwd_in, bwd_grad, seg_fwd, seg_bwd, w_query, w_key, gain, gossip_exp):
    query_weight = w_query[0, 0]
    key_weight = w_key[0, 0]
    gain_own = gain[0, 0].reshape(1, -1)
    grad_rows = bwd_grad[0, 0]
    count, local = grad_rows.shape
    width = 2 * local
    pipe_count = lax.axis_size("pipe")
    rep_count = lax.axis_size("rep")
    levels = rep_count.bit_length() - 1
    at = lax.axis_index("tp").astype(jnp.int32).reshape(1)
    exponent = gossip_exp[0]

    bwd_other = shifted(bwd_in[0, 0], "tp", 1)
    gain_other = shifted(gain_own, "tp", 1)
    gain_other, fwd_rows = lax.optimization_barrier((gain_other, fwd_in[0, 0]))
    fwd_other = shifted(fwd_rows, "tp", 1)

    q, k, normed, xhat, inv = project(
        at, (bwd_in[0, 0], bwd_other, fwd_in[0, 0], fwd_other), gain_own, gain_other, query_weight, key_weight
    )
    first_rows, last_rows = forward(at, q, k, normed, fwd_in[0, 0], seg_fwd[0, 0])
    q, first_rows, last_rows = lax.optimization_barrier((q, first_rows, last_rows))
    first_rows = shifted(first_rows, "pipe", 1)
    dq, dv, key_part = backward(at, q, k, normed, grad_rows, seg_bwd[0, 0])
    dq, first_rows, last_rows = lax.optimization_barrier((dq, first_rows, last_rows))
    last_rows = shifted(last_rows, "pipe", 1)
    key_other = shifted(key_part.astype(BF16), "tp", 1)
    inward = shifted(away(at, dq, query_weight), "tp", 1)
    dk = (key_part + key_other.astype(F32)).astype(BF16)
    part, gram = home(at, dq, query_weight, dv, dk, key_weight, normed)
    weighted, sums, grad_gain, squares = gather(part, inward, xhat, gain_own, gram)
    last_rows, squares = lax.optimization_barrier((last_rows, squares))
    squares = total_over(squares, "tp")

    bit = jnp.left_shift(gossip_exp, lax.axis_index("pipe").astype(jnp.int32)).astype(F32)
    totals = total_over(jnp.concatenate([squares, bit.reshape(1, 1)], axis=1), "pipe")
    total = pipe_count * (width * width + width * HEAD + width)
    inverse = lax.rsqrt(totals[:, 0:1] / total + STEP_EPS)
    plans = [straight(k, rep_count, pipe_count) for k in range(levels)]
    if rep_count == 4 and pipe_count == 4:
        plans += [crossed(bit, far, rep_count, pipe_count) for bit in range(2) for far in range(2)]
        table = [choices([n >> p & 1 for p in range(pipe_count)]) for n in range(1 << pipe_count)]
        own = jnp.asarray(table, jnp.int32)
        place = totals[0, 1].astype(jnp.int32) * pipe_count + lax.axis_index("pipe")
        exponent = jnp.sum(jnp.where(jnp.arange(own.size) == place, own.reshape(-1), 0))

    back_rows = turn(weighted, xhat, inv, sums, shifted(sums, "tp", 1), grad_rows)
    back_rows, inverse = lax.optimization_barrier((back_rows, inverse))
    prev_rows = shifted(back_rows, "pipe", -1)
    early = step(normed, dq, query_weight, inverse, 0, 2 * width // PIECES)
    values = (at, early, normed, dq, query_weight, dk, key_weight, gain_own, grad_gain, inverse)
    values += (first_rows, last_rows)
    query_out, key_out, gain_out, next_rows = lax.switch(exponent, [partial(swap, plan=plan) for plan in plans], values)
    outs = (next_rows, prev_rows, query_out, key_out, gain_out)
    return tuple(out[None, None] for out in outs)


def solution(mesh):
    rows = P("rep", "pipe", None, "tp")
    tokens = P("rep", "pipe", None)
    keyed = P("rep", "pipe", None, None)
    line = P("rep", "pipe", "tp")
    return jax.shard_map(
        shards,
        mesh=mesh,
        in_specs=(rows, rows, rows, tokens, tokens, rows, keyed, line, P("pipe")),
        out_specs=(rows, rows, rows, keyed, line),
        check_vma=False,
    )
```
